32 devices in a mesh: grp: 2 (over y), kz: 4 (over z), coil: 2 (over x), kx: 2 (over core).
Axes of the slice: x: 2, y: 2, z: 4, core: 2. Of those that a mesh axis runs over, the one named last changes fastest.
Arguments:
- measured: float32 [2, 64, 32, 32, 32], P(None, ('grp', 'coil'), 'kx', 'kz'), parts along dimension 1, may hold values from -6 to 6
- mask: int32 [64, 32, 32], P(('grp', 'kx'), 'kz'), parts along dimension 0, may hold values 0 or 1
- kernel: float32 [27, 2, 32, 64], P(None, None, 'coil'), may hold values from -0.109375 to 0.109375
Outputs:
- restored: float32 [2, 64, 32, 32, 32], P(None, ('grp', 'coil'), 'kx', 'kz'), parts along dimension 1
The draws below stay inside these ranges and needn't reach their ends.
There are 2 independent parts, one for each index of `grp`. The reference program is written for one: setup_inputs(seed, part) draws one part's arguments, and reference() takes and returns one part's arrays. A program takes and returns all parts, laid end to end along the dimension named above; an argument that names none is the same for every part. Nothing has to cross between parts.
All inputs are finite; a program needn't handle non-finite values. No bound on the sum of `mask` on one device may be relied on, other than what follows from the above.
Results may differ from the reference program's by a relative error of at most 0.0001.
Values sent between devices are 32-bit elements; how exact they have to be, the bound alone decides.
No kernel may reach another device: no remote copies, remote signals or barrier semaphores. Data moves between devices by JAX's collectives and lax.ppermute only.
A program may use at most 128 MiB of HBM per device.

```python
import jax
import jax.numpy as jnp
from jax import lax

COILS = 32
KX = 32
KY = 32
ITERS = 2
TAPS = 27
KZ = 32


def touch_ends(drawn, rng, low, largest):
    longest = drawn.shape.index(max(drawn.shape))
    spots = []
    for shift in (0, 1):
        where = [jax.random.randint(jax.random.fold_in(rng, axis), (), 0, length) for axis, length in enumerate(drawn.shape)]
        where[longest] = (where[longest] + shift) % drawn.shape[longest]
        spots.append(tuple(where))
    return drawn.at[spots[0]].set(low).at[spots[1]].set(largest)


def steps_of(own_key, shape, shards, low, high):
    loudness = 1.0
    for position, parts in shards:
        heights = jax.random.uniform(jax.random.fold_in(jax.random.fold_in(own_key, 6), position), (parts,), jnp.float32, low / len(shards), high / len(shards))
        loudness = loudness * jnp.repeat(jnp.exp(heights), shape[position] // parts).reshape((-1,) + (1,) * (len(shape) - 1 - position))
    return loudness


def bell_draw(key, extent, width, bound, shards=(), kind=jnp.bfloat16):
    entries = jax.random.normal(key, extent, jnp.float32) * width
    if len(shards) > 0:
        entries = steps_of(key, extent, shards, -0.22, 0.18) * entries
    return jnp.clip(entries, min=-bound, max=bound).astype(kind)


def setup_inputs(seed: int = 0, part: int = 0) -> dict:
    key_list = jax.random.split(jax.random.key(seed), 4)
    part_keys = jax.random.split(jax.random.fold_in(key_list[3], part), 4)
    measured = bell_draw(part_keys[0], (2, COILS, KX, KZ, KY), 1.0, 6.0, ((1, 2), (2, 2), (3, 4)), jnp.float32)
    mask = touch_ends((jax.random.randint(part_keys[1], (KX, KZ, KY), 0, 2) < 1).astype(jnp.int32), jax.random.fold_in(part_keys[1], 1), 0, 1)
    kernel = bell_draw(key_list[2], (TAPS, 2, COILS, 2 * COILS), (108 * COILS) ** -0.5, 0.109375, ((2, 2),), jnp.float32)
    return {"measured": measured, "mask": mask, "kernel": kernel}


def reference(measured, mask, kernel):
    sampled = (mask == 1)[None, None]
    state = jnp.where(sampled, measured, jnp.zeros_like(measured))
    real_k = kernel[:, 0]
    imag_k = kernel[:, 1]
    weights = jnp.concatenate([jnp.concatenate([real_k, -imag_k], 2), jnp.concatenate([imag_k, real_k], 2)], 1)
    sign = jnp.array([1.0, -1.0], jnp.float32).reshape(2, 1, 1, 1, 1)
    for step in range(ITERS):
        virtual = jnp.flip(state, (2, 3, 4)) * sign
        stacked = jnp.concatenate([state, virtual], 1)
        padded = jnp.pad(stacked, ((0, 0), (0, 0), (1, 1), (1, 1), (1, 1)))
        result = jnp.zeros(state.shape, jnp.float32)
        for first in range(3):
            for second in range(3):
                for third in range(3):
                    window = padded[:, :, first:first + KX, third:third + KZ, second:second + KY]
                    window = window.reshape(4 * COILS, -1)
                    term = jnp.dot(weights[9 * first + 3 * second + third], window, precision=lax.Precision.HIGHEST)
                    result = result + term.reshape(state.shape)
        state = jnp.where(sampled, measured, result)
    return state
```

```python
import functools

import jax
import jax.numpy as jnp
from jax import lax
from jax.experimental import pallas as pl
from jax.experimental.pallas import tpu as pltpu
from jax.sharding import PartitionSpec as P

ITERS = 2
F32 = jnp.float32
BF16 = jnp.bfloat16
PARAMS = pltpu.CompilerParams(vmem_limit_bytes=48 << 20)
SMEM = pl.BlockSpec(memory_space=pltpu.SMEM)
VMEM = pl.BlockSpec(memory_space=pltpu.VMEM)


def split(x):
    hi = x.astype(BF16)
    return hi, (x - hi.astype(F32)).astype(BF16)


def reversal(n):
    row = lax.broadcasted_iota(jnp.int32, (n, n), 0)
    column = lax.broadcasted_iota(jnp.int32, (n, n), 1)
    return jnp.where(row + column == n - 1, 1.0, 0.0).astype(BF16)


def dot(a, b):
    return jnp.dot(a, b, preferred_element_type=F32)


def reversed_rows(x):
    hi, lo = split(x)
    flip = reversal(x.shape[0])
    return dot(flip, hi) + dot(flip, lo)


def pack_kernel(C, R, c_ref, measured, mask, *outs):
    c = c_ref[0]
    ch, _, D, W = measured.shape
    for d in range(C):
        for side in range(2):
            piece = lax.bitwise_xor(c, d)
            if side:
                piece = 2 * C - 1 - piece
            rows, marks = [], []
            for j in range(R):
                mark = mask[piece * R + j] == 1
                marks.append(jnp.where(mark, 1.0, 0.0))
                rows.append(jnp.where(mark[None], measured[:, piece * R + j], 0.0))
            out = outs[2 * d + side]
            out[: ch * D] = jnp.concatenate(rows, -1).reshape(ch * D, R * W)
            if d == 0:
                out[ch * D :] = jnp.concatenate(marks, -1)


def pack(c, measured, mask, C, R):
    ch, _, D, W = measured.shape
    shapes = []
    for d in range(C):
        shapes += [jax.ShapeDtypeStruct((ch * D + (D if d == 0 else 0), R * W), F32)] * 2
    return pl.pallas_call(
        functools.partial(pack_kernel, C, R),
        out_shape=shapes,
        in_specs=[SMEM, VMEM, VMEM],
        out_specs=[VMEM] * len(shapes),
        compiler_params=PARAMS,
        name="pack",
    )(c, measured, mask)


def weights_kernel(coils, kernel, w_hi, w_lo):
    taps = kernel.shape[0]

    def step(t, carry):
        def parts(tap):
            re, im = kernel[tap, 0], kernel[tap, 1]
            return re[:, :coils], im[:, :coils], re[:, coils:], im[:, coils:]

        pr, pi, vr, vi = parts(t)
        qr, qi, ur, ui = parts(taps - 1 - t)
        block = jnp.concatenate(
            [
                jnp.concatenate([pr, -pi, vr, vi], 1),
                jnp.concatenate([pi, pr, vi, -vr], 1),
                jnp.concatenate([ur, ui, qr, -qi], 1),
                jnp.concatenate([ui, -ur, qi, qr], 1),
            ],
            0,
        ).T
        hi, lo = split(block)
        first, second, third = t // 9, (t // 3) % 3, t % 3
        w_hi[second, first * 3 + third] = hi
        w_lo[second, first * 3 + third] = lo
        return carry

    lax.fori_loop(0, taps, step, 0)


def build_weights(kernel):
    taps, _, coils, _ = kernel.shape
    shape = jax.ShapeDtypeStruct((3, taps // 3, 4 * coils, 4 * coils), BF16)
    return pl.pallas_call(
        functools.partial(weights_kernel, coils),
        out_shape=[shape, shape],
        in_specs=[VMEM],
        out_specs=[VMEM, VMEM],
        compiler_params=PARAMS,
        name="weights",
    )(kernel)


def points_kernel(C, R, D, W, half, c_ref, *refs):
    msgs, (x, marks, stage) = refs[: 2 * C], refs[2 * C :]
    c = c_ref[0]
    size = msgs[1 if C > 1 else 0].shape[0]
    ch = 2 * (half // (2 * C))
    part = (ch // 2) * D
    for d in range(C):
        for side in range(2):
            for ri in range(2):
                start = ((side * 2 + ri) * C + lax.bitwise_xor(c, d)) * part
                start = pl.multiple_of(start, part)
                stage[pl.ds(start, part)] = msgs[2 * d + side][ri * part : (ri + 1) * part]
    L = R * W
    lane = lax.broadcasted_iota(jnp.int32, (L, 2 * half), 1)
    own_marks = msgs[0][ch * D :]
    other_marks = msgs[1][ch * D :]
    pad = jnp.zeros((2 * half - D, L), F32)
    own_marks = jnp.concatenate([own_marks, pad], 0).T
    other_marks = reversed_rows(jnp.concatenate([other_marks, pad], 0).T)
    for k in range(D):
        mine = stage[pl.ds(k, half, stride=D)]
        other = stage[pl.ds(half * D + D - 1 - k, half, stride=D)]
        both = jnp.concatenate([mine, other], 0).T
        both = jnp.where(lane < half, both, reversed_rows(both))
        mark = jnp.where(lane < half, own_marks[:, k : k + 1], other_marks[:, D - 1 - k : D - k])
        for i in range(R):
            x[i, k * W : (k + 1) * W] = both[i * W : (i + 1) * W]
            marks[i, k * W : (k + 1) * W] = mark[i * W : (i + 1) * W]


def points(c, msgs, C, R, D, W, half):
    shape = jax.ShapeDtypeStruct((R, D * W, 2 * half), F32)
    return pl.pallas_call(
        functools.partial(points_kernel, C, R, D, W, half),
        out_shape=[shape, shape],
        in_specs=[SMEM] + [VMEM] * len(msgs),
        out_specs=[VMEM, VMEM],
        scratch_shapes=[pltpu.VMEM((2 * half * D, R * W), F32)],
        compiler_params=PARAMS,
        name="points",
    )(c, *msgs)


def convolve(C, R, D, W, c, x, before, after, natural, mirrored, w_hi, w_lo, hi, lo):
    half = x.shape[-1] // 2

    def put(i, rows, value):
        h, l = split(value)
        hi[i, rows] = h
        lo[i, rows] = l

    inner, low, high = slice(W, (D + 1) * W), slice(0, W), slice((D + 1) * W, (D + 2) * W)
    for i in range(R):
        put(i + 1, low, before[i * W : (i + 1) * W])
        put(i + 1, inner, x[i])
        put(i + 1, high, after[i * W : (i + 1) * W])
    odd = lax.rem(c, 2)
    put((1 - odd) * (R + 1), slice(None), natural[...])
    face = mirrored[...]
    flipped = pltpu.roll(reversed_rows(face), half, 1)
    if C > 2:
        flipped = jnp.where(jnp.logical_or(c == 0, c == C - 1), flipped, face)
    put(odd * (R + 1), slice(None), flipped)

    def window(ref):
        return jnp.concatenate(
            [
                jnp.concatenate([ref[i + a, e * W : (e + D) * W] for i in range(R)], 0)
                for a in range(3)
                for e in range(3)
            ],
            1,
        )

    wide = jnp.concatenate([window(hi), window(lo), window(hi)], 1)
    rows = lax.broadcasted_iota(jnp.int32, (R * D * W, 2 * half), 0) % W
    total = None
    for b in range(3):
        own_hi = w_hi[b].reshape(-1, 2 * half)
        own_lo = w_lo[b].reshape(-1, 2 * half)
        y = dot(wide, jnp.concatenate([own_hi, own_hi, own_lo], 0))
        if b == 0:
            y = jnp.where(rows == 0, 0.0, pltpu.roll(y, 1, 0))
        if b == 2:
            y = jnp.where(rows == W - 1, 0.0, pltpu.roll(y, R * D * W - 1, 0))
        total = y if total is None else total + y
    return total.reshape(R, D * W, 2 * half)


def middle_kernel(C, R, D, W, c_ref, x, marks, before, after, natural, mirrored, w_hi, w_lo, out, hi, lo):
    y = convolve(C, R, D, W, c_ref[0], x, before, after, natural, mirrored, w_hi, w_lo, hi, lo)
    out[...] = jnp.where(marks[...] > 0.5, x[...], y)


def last_kernel(C, R, D, W, c_ref, x, before, after, natural, mirrored, w_hi, w_lo, *rest):
    outs, (hi, lo, stage) = rest[: 2 * C], rest[2 * C :]
    c = c_ref[0]
    y = convolve(C, R, D, W, c, x, before, after, natural, mirrored, w_hi, w_lo, hi, lo)
    half = x.shape[-1] // 2
    flip = reversal(R * W)
    for k in range(D):
        rows = jnp.concatenate([y[i, k * W : (k + 1) * W] for i in range(R)], 0).T
        stage[pl.ds(k, half, stride=D)] = rows[:half]
        h, l = split(rows[half:])
        stage[pl.ds(half * D + D - 1 - k, half, stride=D)] = dot(h, flip) + dot(l, flip)
    part = (half // (2 * C)) * D
    for d in range(C):
        for side in range(2):
            for ri in range(2):
                start = ((side * 2 + ri) * C + lax.bitwise_xor(c, d)) * part
                start = pl.multiple_of(start, part)
                outs[2 * d + side][ri * part : (ri + 1) * part] = stage[pl.ds(start, part)]


def iterate(last, c, x, marks, halos, weights, C, R, D, W):
    channels = x.shape[-1]
    scratch = [pltpu.VMEM((R + 2, (D + 2) * W, channels), BF16)] * 2
    if last:
        message = jax.ShapeDtypeStruct((channels // (2 * C) * D, R * W), F32)
        shapes = [message] * (2 * C)
        scratch.append(pltpu.VMEM((channels * D, R * W), F32))
        body, args = last_kernel, (c, x, *halos, *weights)
    else:
        shapes = [jax.ShapeDtypeStruct(x.shape, F32)]
        body, args = middle_kernel, (c, x, marks, *halos, *weights)
    return pl.pallas_call(
        functools.partial(body, C, R, D, W),
        out_shape=shapes,
        in_specs=[SMEM] + [VMEM] * (len(args) - 1),
        out_specs=[VMEM] * len(shapes),
        scratch_shapes=scratch,
        compiler_params=PARAMS,
        name="last" if last else "middle",
    )(*args)


def unpack_kernel(C, R, c_ref, measured, mask, *refs):
    msgs, out = refs[: 2 * C], refs[2 * C]
    c = c_ref[0]
    ch, _, D, W = measured.shape
    for d in range(C):
        for side in range(2):
            piece = lax.bitwise_xor(c, d)
            if side:
                piece = 2 * C - 1 - piece
            msg = msgs[2 * d + side][...].reshape(ch, D, R * W)
            for j in range(R):
                row = piece * R + j
                out[:, row] = jnp.where((mask[row] == 1)[None], measured[:, row], msg[:, :, j * W : (j + 1) * W])


def unpack(c, measured, mask, msgs, C, R):
    return pl.pallas_call(
        functools.partial(unpack_kernel, C, R),
        out_shape=jax.ShapeDtypeStruct(measured.shape, F32),
        in_specs=[SMEM] + [VMEM] * (2 + len(msgs)),
        out_specs=VMEM,
        compiler_params=PARAMS,
        name="unpack",
    )(c, measured, mask, *msgs)


def on_device(measured, mask, kernel):
    Z, C, X = lax.axis_size("kz"), lax.axis_size("coil"), lax.axis_size("kx")
    axes = ("kz", "coil", "kx")
    every = [(z, c, x) for z in range(Z) for c in range(C) for x in range(X)]

    def index(z, c, x):
        return (z * C + c) * X + x

    def send(array, target):
        pairs = [(index(*p), index(*target(*p))) for p in every if target(*p) is not None]
        return lax.ppermute(array, axes, pairs)

    def exchange(msgs):
        got = list(msgs)
        for d in reversed(range(C)):
            got[2 * d + 1] = send(msgs[2 * d + 1], lambda z, c, x: (Z - 1 - z, c ^ d, X - 1 - x))
        for d in range(1, C):
            got[2 * d] = send(msgs[2 * d], lambda z, c, x: (z, c ^ d, x))
        return got

    def across(z, c, x):
        if c % 2:
            return (z, c + 1, x) if c + 1 < C else (Z - 1 - z, c, X - 1 - x)
        if c:
            return (z, c - 1, x)
        return (Z - 1 - z, c, X - x) if x else None

    parts, coils, rows, D, W = measured.shape
    R = rows // (2 * C)
    half = parts * coils * C
    coil = lax.axis_index("coil")
    c = coil.astype(jnp.int32).reshape(1)
    odd = coil % 2 == 1
    flat = measured.reshape(parts * coils, rows, D, W)

    msgs = exchange(pack(c, flat, mask, C, R))
    weights = build_weights(lax.all_gather(kernel, "coil", axis=2, tiled=True))
    x, marks = points(c, msgs, C, R, D, W, half)
    for step in range(ITERS):
        first = x[:, :W].reshape(R * W, 2 * half)
        final = x[:, (D - 1) * W :].reshape(R * W, 2 * half)
        before = send(final, lambda z, c, x: (z + 1, c, x) if z + 1 < Z else None)
        after = send(first, lambda z, c, x: (z - 1, c, x) if z else None)

        def face(i):
            return jnp.concatenate([before[i * W : (i + 1) * W], x[i], after[i * W : (i + 1) * W]], 0)

        lower, upper = face(0), face(R - 1)
        natural = send(jnp.where(odd, lower, upper), lambda z, c, x: (z, c ^ 1, x))
        mirrored = send(jnp.where(odd, upper, lower), across)
        out = iterate(step == ITERS - 1, c, x, marks, (before, after, natural, mirrored), weights, C, R, D, W)
        if step < ITERS - 1:
            x = out[0]
    return unpack(c, flat, mask, exchange(out), C, R).reshape(measured.shape)


def solution(mesh):
    placed = (
        P(None, ("grp", "coil"), "kx", "kz", None),
        P(("grp", "kx"), "kz", None),
        P(None, None, "coil", None),
    )
    return jax.shard_map(
        on_device,
        mesh=mesh,
        in_specs=placed,
        out_specs=P(None, ("grp", "coil"), "kx", "kz", None),
        check_vma=False,
    )
```

```python
import functools

import jax
import jax.numpy as jnp
from jax import lax
from jax.experimental import pallas as pl
from jax.experimental.pallas import tpu as pltpu
from jax.sharding import PartitionSpec as P

ITERS = 2
AXES = ("kz", "coil", "kx")
F32 = jnp.float32
BF16 = jnp.bfloat16
PARAMS = pltpu.CompilerParams(vmem_limit_bytes=48 << 20)
ANY = pl.BlockSpec(memory_space=pl.ANY)
HBM = pl.BlockSpec(memory_space=pltpu.HBM)
VMEM = pl.BlockSpec(memory_space=pltpu.VMEM)


def call(body, name, args, shapes, scratch=(), far=(), space=ANY, out=VMEM, **options):
    return pl.pallas_call(
        body,
        out_shape=shapes,
        in_specs=[space if i in far else VMEM for i in range(len(args))],
        out_specs=[out] * len(shapes),
        scratch_shapes=list(scratch),
        compiler_params=PARAMS,
        name=name,
        **options,
    )(*args)


def split(x):
    hi = x.astype(BF16)
    return hi, (x - hi.astype(F32)).astype(BF16)


def reversal(n):
    row = lax.broadcasted_iota(jnp.int32, (n, n), 0)
    column = lax.broadcasted_iota(jnp.int32, (n, n), 1)
    return jnp.where(row + column == n - 1, 1.0, 0.0).astype(BF16)


def dot(a, b):
    return jnp.dot(a, b, preferred_element_type=F32)


def reversed_rows(x):
    hi, lo = split(x)
    flip = reversal(x.shape[0])
    return dot(flip, hi) + dot(flip, lo)


def is_upper(z, x, Z):
    return (x == 0) != (z >= Z // 2)


def place():
    return tuple(lax.axis_index(axis) for axis in AXES)


def piece_of(C, d, side):
    z, c, x = place()
    upper = jnp.where(is_upper(z, x, lax.axis_size("kz")), C, 0)
    piece = lax.bitwise_xor(c, d) + upper
    return 2 * C - 1 - piece if side else piece


def pack_kernel(C, R, measured, mask, *refs):
    outs, (rows, marks, sems) = refs[: 2 * C], refs[2 * C :]
    ch, _, D, W = measured.shape
    copies = [pltpu.make_async_copy(mask, marks, sems.at[2 * C])]
    order = [(side, d) for side in (1, 0) for d in range(C)]
    for slot, (side, d) in enumerate(order):
        start = piece_of(C, d, side) * R
        copies.append(pltpu.make_async_copy(measured.at[:, pl.ds(start, R)], rows.at[slot], sems.at[slot]))
    for copy in copies:
        copy.start()
    copies[0].wait()
    for slot, (side, d) in enumerate(order):
        copies[slot + 1].wait()
        start = piece_of(C, d, side) * R
        sampled = [marks[start + j] == 1 for j in range(R)]
        kept = [jnp.where(sampled[j][None], rows[slot, :, j], 0.0) for j in range(R)]
        out = outs[2 * d + side]
        out[: ch * D] = jnp.concatenate(kept, -1).reshape(ch * D, R * W)
        if d == 0:
            out[ch * D :] = jnp.concatenate([jnp.where(s, 1.0, 0.0) for s in sampled], -1)


def pack(measured, mask, C, R):
    ch, _, D, W = measured.shape
    shapes = []
    for d in range(C):
        shapes += [jax.ShapeDtypeStruct((ch * D + (D if d == 0 else 0), R * W), F32)] * 2
    scratch = [
        pltpu.VMEM((2 * C, ch, R, D, W), F32),
        pltpu.VMEM(mask.shape, jnp.int32),
        pltpu.SemaphoreType.DMA((2 * C + 1,)),
    ]
    return call(functools.partial(pack_kernel, C, R), "pack", (measured, mask), shapes, scratch, far=(0, 1), space=HBM)


def fold_kernel(kernel, out):
    half = kernel.shape[2] // 2
    out[...] = jnp.concatenate([kernel[:, :, :half], kernel[:, :, half:]], -1)


def weights_kernel(C, *refs):
    folded, (single, double, kernel) = refs[:C], refs[C:]
    taps, _, coils, inputs = kernel.shape
    half = folded[0].shape[2]
    for d in range(C):
        start = pl.multiple_of(lax.bitwise_xor(lax.axis_index("coil"), d) * 2 * half, 2 * half)
        kernel[:, :, pl.ds(start, half)] = folded[d][..., :inputs]
        kernel[:, :, pl.ds(start + half, half)] = folded[d][..., inputs:]

    def parts(tap):
        re, im = kernel[tap, 0], kernel[tap, 1]
        return re[:, :coils], im[:, :coils], re[:, coils:], im[:, coils:]

    N = 4 * coils
    for t in range(taps):
        pr, pi, vr, vi = parts(t)
        qr, qi, ur, ui = parts(taps - 1 - t)
        block = jnp.concatenate(
            [
                jnp.concatenate([pr, -pi, vr, vi], 1),
                jnp.concatenate([pi, pr, vi, -vr], 1),
                jnp.concatenate([ur, ui, qr, -qi], 1),
                jnp.concatenate([ui, -ur, qi, qr], 1),
            ],
            0,
        ).T
        hi, lo = split(block)
        b, tap = (t // 3) % 3, t // 9 * 3 + t % 3
        single[tap, :, b * N : (b + 1) * N] = hi
        double[tap, :, 2 * b * N : (2 * b + 1) * N] = hi
        double[tap, :, (2 * b + 1) * N : (2 * b + 2) * N] = lo


def build_weights(C, folded, coils):
    taps, parts, _, inputs = folded[0].shape
    N = 4 * coils
    shapes = [jax.ShapeDtypeStruct((9, N, 3 * N), BF16), jax.ShapeDtypeStruct((9, N, 6 * N), BF16)]
    scratch = [pltpu.VMEM((taps, parts, coils, inputs // 2), F32)]
    return call(functools.partial(weights_kernel, C), "weights", folded, shapes, scratch)


def plane_faces(x, face_a, face_b):
    R, rows, channels = x.shape
    W = face_a.shape[0] // R
    z, Z = lax.axis_index("kz"), lax.axis_size("kz")
    first = x[:, :W].reshape(R * W, channels)
    final = x[:, rows - W :].reshape(R * W, channels)
    odd = lax.rem(z, 2) == 1
    face_a[...] = jnp.where(odd, first, final)
    face = jnp.where(odd, final, first)
    flipped = pltpu.roll(reversed_rows(face), channels // 2, 1)
    face_b[...] = jnp.where(jnp.logical_or(z == Z // 2 - 1, z == Z // 2), flipped, face)


def points_kernel(C, R, D, W, half, ready, *refs):
    msgs, (x, marks, face_a, face_b, stage) = refs[: 2 * C], refs[2 * C :]
    c = lax.axis_index("coil")
    ch = half // C
    part = (ch // 2) * D
    for d in range(C):
        for side in range(2):
            for ri in range(2):
                start = ((side * 2 + ri) * C + lax.bitwise_xor(c, d)) * part
                start = pl.multiple_of(start, part)
                stage[pl.ds(start, part)] = msgs[2 * d + side][ri * part : (ri + 1) * part]
    L = R * W
    lane = lax.broadcasted_iota(jnp.int32, (L, 2 * half), 1)
    pad = jnp.zeros((2 * half - D, L), F32)
    own_marks = jnp.concatenate([msgs[0][ch * D :], pad], 0).T
    other_marks = reversed_rows(jnp.concatenate([msgs[1][ch * D :], pad], 0).T)
    for k in range(D):
        mine = stage[pl.ds(k, half, stride=D)]
        other = stage[pl.ds(half * D + D - 1 - k, half, stride=D)]
        both = jnp.concatenate([mine, other], 0).T
        both = jnp.where(lane < half, both, reversed_rows(both))
        mark = jnp.where(lane < half, own_marks[:, k : k + 1], other_marks[:, D - 1 - k : D - k])
        for i in range(R):
            x[i, k * W : (k + 1) * W] = both[i * W : (i + 1) * W]
            marks[i, k * W : (k + 1) * W] = mark[i * W : (i + 1) * W]
    plane_faces(x, face_a, face_b)


def points(ready, msgs, C, R, D, W, half):
    shape = jax.ShapeDtypeStruct((R, D * W, 2 * half), F32)
    face = jax.ShapeDtypeStruct((R * W, 2 * half), F32)
    return call(
        functools.partial(points_kernel, C, R, D, W, half),
        "points",
        (ready, *msgs),
        [shape, shape, face, face],
        [pltpu.VMEM((2 * half * D, R * W), F32)],
        far=(0,),
    )


def multiply(hi, lo, single, double, W):
    M, N = hi.shape[0], single.shape[-1] // 3
    y, z = dot(hi, double), dot(lo, single)
    y = [
        y[:, 2 * b * N : (2 * b + 1) * N] + y[:, (2 * b + 1) * N : (2 * b + 2) * N] + z[:, b * N : (b + 1) * N]
        for b in range(3)
    ]
    rows = lax.broadcasted_iota(jnp.int32, (M, N), 0) % W
    right = jnp.where(rows == 0, 0.0, pltpu.roll(y[0], 1, 0))
    left = jnp.where(rows == W - 1, 0.0, pltpu.roll(y[2], M - 1, 0))
    return y[1] + right + left


def taps_of(weights, a, e):
    return [jnp.concatenate([w[3 * i + j] for i in a for j in e], 0) for w in weights]


def own_part(R, D, W, start, count, x, weights, hi, lo):
    channels = x.shape[-1]
    edge = jnp.zeros((W, channels), BF16)
    for j in range(count + 2):
        row = start + j - 1
        if 0 <= row < R:
            hi[j, W : (D + 1) * W], lo[j, W : (D + 1) * W] = split(x[row])
            for ref in (hi, lo):
                ref[j, :W] = edge
                ref[j, (D + 1) * W :] = edge
        else:
            hi[j] = lo[j] = jnp.zeros(((D + 2) * W, channels), BF16)

    def window(ref):
        return jnp.concatenate(
            [
                jnp.concatenate([ref[i + a, e * W : (e + D) * W] for i in range(count)], 0)
                for a in range(3)
                for e in range(3)
            ],
            1,
        )

    y = multiply(window(hi), window(lo), *taps_of(weights, range(3), range(3)), W)
    return y.reshape(count, D * W, channels)


def upper_kernel(R, D, W, x, single, double, out, hi, lo):
    out[...] = own_part(R, D, W, 0, out.shape[0], x, (single, double), hi, lo)


def lower_kernel(R, D, W, x, upper, before, after, single, double, out, hi, lo):
    weights = (single, double)
    count = upper.shape[0]
    out[:count] = upper[...]
    out[count:] = own_part(R, D, W, count, R - count, x, weights, hi, lo)
    edge = jnp.zeros((W, x.shape[-1]), BF16)
    for plane, e, k in ((before, 0, 0), (after, 2, D - 1)):
        wide = [
            jnp.concatenate(
                [jnp.concatenate([edge, part[:-W]], 0), part, jnp.concatenate([part[W:], edge], 0)], 1
            )
            for part in split(plane[...])
        ]
        y = multiply(*wide, *taps_of(weights, range(3), [e]), W)
        for i in range(R):
            out[i, k * W : (k + 1) * W] += y[i * W : (i + 1) * W]


def finish(D, W, main, near, far, weights):
    R, _, channels = main.shape
    z, c, x = place()
    C = lax.axis_size("coil")
    upper = is_upper(z, x, lax.axis_size("kz"))
    mirrored = jnp.where(upper, c == 0, c == C - 1)
    edge = jnp.where(upper, (c == C - 1) & (x == 1), (c == 0) & (x == 0))
    near, far = near[...], far[...]
    far = jnp.where(mirrored, pltpu.roll(reversed_rows(far), channels // 2, 1), far)
    far = jnp.where(edge, 0.0, far)
    odd = lax.rem(c, 2) == 1
    below = jnp.where(odd, near, far)
    above = jnp.where(odd, far, near)
    rows = [main[i] for i in range(R)]
    for plane, a, row in ((below, 0, 0), (above, 2, R - 1)):
        wide = [jnp.concatenate([p[e * W : (e + D) * W] for e in range(3)], 1) for p in split(plane)]
        rows[row] += multiply(*wide, *taps_of(weights, [a], range(3)), W)
    return rows


def middle_kernel(D, W, x, marks, main, near, far, single, double, out, face_a, face_b):
    for i, row in enumerate(finish(D, W, main, near, far, (single, double))):
        out[i] = jnp.where(marks[i] > 0.5, x[i], row)
    plane_faces(out, face_a, face_b)


def last_kernel(C, D, W, main, near, far, single, double, *rest):
    outs, stage = rest[: 2 * C], rest[2 * C]
    y = finish(D, W, main, near, far, (single, double))
    half = main.shape[-1] // 2
    flip = reversal(len(y) * W)
    for k in range(D):
        rows = jnp.concatenate([row[k * W : (k + 1) * W] for row in y], 0).T
        stage[pl.ds(k, half, stride=D)] = rows[:half]
        h, l = split(rows[half:])
        stage[pl.ds(half * D + D - 1 - k, half, stride=D)] = dot(h, flip) + dot(l, flip)
    part = (half // (2 * C)) * D
    for d in range(C):
        for side in range(2):
            for ri in range(2):
                start = ((side * 2 + ri) * C + lax.bitwise_xor(lax.axis_index("coil"), d)) * part
                start = pl.multiple_of(start, part)
                outs[2 * d + side][ri * part : (ri + 1) * part] = stage[pl.ds(start, part)]


def unpack_kernel(C, R, side, measured, mask, *refs):
    msgs, (out, rows, sems) = refs[:C], refs[-3:]
    ch, _, D, W = measured.shape
    copies = []
    for d in range(C):
        start = piece_of(C, d, side) * R
        msg = msgs[d][...].reshape(ch, D, R * W)
        for j in range(R):
            sampled = (mask[start + j] == 1)[None]
            rows[d, :, j] = jnp.where(sampled, measured[:, start + j], msg[:, :, j * W : (j + 1) * W])
        copies.append(pltpu.make_async_copy(rows.at[d], out.at[:, pl.ds(start, R)], sems.at[d]))
        copies[-1].start()
    for copy in copies:
        copy.wait()


def unpack(side, measured, mask, msgs, C, R, into=None):
    ch, _, D, W = measured.shape
    args = (measured, mask, *msgs) + (() if into is None else (into,))
    (out,) = call(
        functools.partial(unpack_kernel, C, R, side),
        "unpack_mirrored" if side else "unpack_own",
        args,
        [jax.ShapeDtypeStruct(measured.shape, F32)],
        [pltpu.VMEM((C, ch, R, D, W), F32), pltpu.SemaphoreType.DMA((C,))],
        far=() if into is None else (len(args) - 1,),
        out=ANY,
        input_output_aliases={} if into is None else {len(args) - 1: 0},
    )
    return out


def on_device(measured, mask, kernel):
    Z, C, X = (lax.axis_size(axis) for axis in AXES)
    every = [(z, c, x) for z in range(Z) for c in range(C) for x in range(X)]

    def index(z, c, x):
        return (z * C + c) * X + x

    def send(array, target):
        pairs = [(index(*p), index(*target(*p))) for p in every if target(*p) is not None]
        return lax.ppermute(array, AXES, pairs)

    def exchange(msgs):
        got = list(msgs)
        for d in range(C):
            got[2 * d + 1] = send(msgs[2 * d + 1], lambda z, c, x: (Z - 1 - z, c ^ d, X - 1 - x))
        for d in range(1, C):
            got[2 * d] = send(msgs[2 * d], lambda z, c, x: (z, c ^ d, x))
        return got

    def plane_a(z, c, x):
        return (z ^ 1, c, x)

    def plane_b(z, c, x):
        other = z + 1 if z % 2 else z - 1
        if {z, other} == {Z // 2 - 1, Z // 2}:
            return (z, C - 1 - c, X - 1 - x)
        return (other, c, x) if 0 <= other < Z else (z, c, X - 1 - x)

    def row_a(z, c, x):
        return (z, c ^ 1, x)

    def row_b(z, c, x):
        other = c + 1 if c % 2 else c - 1
        if 0 <= other < C:
            return (z, other, x)
        if is_upper(z, x, Z) == (other < 0):
            return (Z - 1 - z, c, X - 1 - x)
        return (z, C - 1 - c, X - 1 - x)

    parts, coils, rows, D, W = measured.shape
    R = rows // (2 * C)
    half = parts * coils * C
    flat = measured.reshape(parts * coils, rows, D, W)
    z, c, _ = place()
    z_odd, c_odd = z % 2 == 1, c % 2 == 1

    taps, _, _, inputs = kernel.shape
    (folded,) = call(
        fold_kernel, "fold", (kernel,), [jax.ShapeDtypeStruct((taps, parts, coils // 2, 2 * inputs), F32)]
    )
    msgs = pack(flat, mask, C, R)
    folded, *msgs = lax.optimization_barrier((folded, *msgs))
    msgs = exchange(msgs)
    folded = [folded] + [send(folded, lambda z, c, x: (z, c ^ d, x)) for d in range(1, C)]
    weights = build_weights(C, folded, coils * C)
    state, marks, face_a, face_b = points(weights[0], msgs, C, R, D, W, half)
    full = jax.ShapeDtypeStruct(state.shape, F32)
    face = jax.ShapeDtypeStruct(face_a.shape, F32)
    early = max(R // 4, 1)
    sizes = (R, D, W)

    def padded(count):
        return [pltpu.VMEM((count + 2, (D + 2) * W, 2 * half), BF16)] * 2

    for step in range(ITERS):
        got_a, got_b = send(face_a, plane_a), send(face_b, plane_b)
        part = jax.ShapeDtypeStruct((early, D * W, 2 * half), F32)
        (top,) = call(functools.partial(upper_kernel, *sizes), "upper", (state, *weights), [part], padded(early))
        got_a, got_b, top = lax.optimization_barrier((got_a, got_b, top))
        got_b = jnp.where((z == 0) | (z == Z - 1), 0.0, got_b)
        before, after = jnp.where(z_odd, got_a, got_b), jnp.where(z_odd, got_b, got_a)

        def row(i):
            return jnp.concatenate([before[i * W : (i + 1) * W], state[i], after[i * W : (i + 1) * W]], 0)

        first, final = row(0), row(R - 1)
        near = send(jnp.where(c_odd, first, final), row_a)
        far = send(jnp.where(c_odd, final, first), row_b)
        (main,) = call(
            functools.partial(lower_kernel, *sizes),
            "lower",
            (state, top, before, after, *weights),
            [full],
            padded(R - early),
        )
        if step < ITERS - 1:
            state, face_a, face_b = call(
                functools.partial(middle_kernel, D, W),
                "middle",
                (state, marks, main, near, far, *weights),
                [full, face, face],
            )
    message = jax.ShapeDtypeStruct((2 * half // (2 * C) * D, R * W), F32)
    msgs = call(
        functools.partial(last_kernel, C, D, W),
        "last",
        (main, near, far, *weights),
        [message] * (2 * C),
        [pltpu.VMEM((2 * half * D, R * W), F32)],
    )
    msgs = exchange(msgs)
    out = unpack(0, flat, mask, msgs[0::2], C, R)
    return unpack(1, flat, mask, msgs[1::2], C, R, out).reshape(measured.shape)


def solution(mesh):
    placed = (
        P(None, ("grp", "coil"), "kx", "kz", None),
        P(("grp", "kx"), "kz", None),
        P(None, None, "coil", None),
    )
    return jax.shard_map(
        on_device,
        mesh=mesh,
        in_specs=placed,
        out_specs=P(None, ("grp", "coil"), "kx", "kz", None),
        check_vma=False,
    )
```

```python
import functools

import jax
import jax.numpy as jnp
from jax import lax
from jax.experimental import pallas as pl
from jax.experimental.pallas import tpu as pltpu
from jax.sharding import PartitionSpec as P

ITERS = 2
AXES = ("kz", "coil", "kx")
F32 = jnp.float32
BF16 = jnp.bfloat16
PARAMS = pltpu.CompilerParams(vmem_limit_bytes=48 << 20)
ANY = pl.BlockSpec(memory_space=pl.ANY)
HBM = pl.BlockSpec(memory_space=pltpu.HBM)
VMEM = pl.BlockSpec(memory_space=pltpu.VMEM)


def call(body, name, args, shapes, scratch=(), far=(), space=ANY, out=VMEM, **options):
    return pl.pallas_call(
        body,
        out_shape=shapes,
        in_specs=[space if i in far else VMEM for i in range(len(args))],
        out_specs=[out] * len(shapes),
        scratch_shapes=list(scratch),
        compiler_params=PARAMS,
        name=name,
        **options,
    )(*args)


def split(x):
    hi = x.astype(BF16)
    return hi, (x - hi.astype(F32)).astype(BF16)


def reversal(n):
    row = lax.broadcasted_iota(jnp.int32, (n, n), 0)
    column = lax.broadcasted_iota(jnp.int32, (n, n), 1)
    return jnp.where(row + column == n - 1, 1.0, 0.0).astype(BF16)


def dot(a, b):
    return jnp.dot(a, b, preferred_element_type=F32)


class Cut:
    def __init__(self, rows, D, W, C, channels):
        self.rows, self.D, self.W, self.C = rows, D, W, C
        self.channels = channels
        self.half = channels // 2
        self.ch = self.half // C
        self.G = rows // C
        self.S = min(rows, self.G + (2 if C == 2 else 4))
        self.H = W // 2
        self.V = self.H + 2
        self.base = 128 // self.H
        self.spare = (self.S - self.base) * self.H
        self.part = self.ch // 2 * D
        self.slots = self.S + 2
        self.pitch = -(-(self.V + 1) // 8) * 8

    def piece(self, d=0):
        c, x = lax.bitwise_xor(lax.axis_index("coil"), d), lax.axis_index("kx")
        return jnp.where(x == 0, c, self.C - 1 - c)

    def start(self, d=0):
        return jnp.clip(self.G * self.piece(d) - 2, 0, self.rows - self.S)

    def range_of(self, last):
        own = self.G * self.piece() - self.start()
        if last:
            return own, self.G
        count = min(self.S, self.G + (1 if self.C == 2 else 2))
        return jnp.clip(own - 1, 0, self.S - count), count


def place():
    return tuple(lax.axis_index(axis) for axis in AXES)


def arrangement(cut):
    S, H, W = cut.S, cut.H, cut.W
    shift = H.bit_length() - 1
    j = lax.broadcasted_iota(jnp.int32, (1, 384), 1)
    own = j - jnp.where(j >= 320, 320, jnp.where(j >= 256, 256, jnp.where(j >= 128, 128, 0)))
    spare = j >= 256
    row = lax.shift_right_logical(own, shift)
    main = row * W + lax.bitwise_and(own, H - 1)
    rest = own - cut.spare
    edge = lax.shift_right_logical(rest, 1) * W + H + lax.bitwise_and(rest, 1)
    source = jnp.where(spare, jnp.where(own < cut.spare, main + cut.base * W, edge), main)
    mirrored = jnp.logical_or(jnp.logical_and(j >= 128, j < 256), j >= 320)
    source = jnp.where(mirrored, S * W - 1 - source, source)
    source = jnp.where(jnp.logical_and(spare, rest >= 2 * S), -1, source)
    lane = lax.broadcasted_iota(jnp.int32, (S * W, 384), 0)
    return jnp.where(lane == source, 1.0, 0.0).astype(BF16)


def pack_kernel(cut, measured, mask, *refs):
    C, S, ch, D, W = cut.C, cut.S, cut.ch, cut.D, cut.W
    outs, (rows, marks, sems) = refs[: 2 * C], refs[2 * C :]
    copies = [pltpu.make_async_copy(mask, marks, sems.at[C])]
    for d in range(C):
        copies.append(pltpu.make_async_copy(measured.at[:, pl.ds(cut.start(d), S)], rows.at[d], sems.at[d]))
    for copy in copies:
        copy.start()
    order = arrangement(cut)
    copies[0].wait()
    for d in range(C):
        copies[d + 1].wait()
        sampled = [marks[cut.start(d) + j] == 1 for j in range(S)]
        kept = [jnp.where(sampled[j][None], rows[d, :, j], 0.0) for j in range(S)]
        kept = jnp.concatenate(kept, -1).reshape(ch * D, S * W)
        if d == 0:
            kept = jnp.concatenate([kept, jnp.concatenate([jnp.where(s, 1.0, 0.0) for s in sampled], -1)], 0)
        hi, lo = split(kept)
        y = dot(hi, order) + dot(lo, order)
        part = cut.part
        for side in range(2):
            out = outs[2 * d + side]
            spare = y[:, 256 + 64 * side : 320 + 64 * side]
            out[: 2 * part] = y[: 2 * part, 128 * side : 128 * side + 128]
            out[2 * part : 3 * part] = jnp.concatenate([spare[:part], spare[part : 2 * part]], 1)
            if d == 0:
                out[3 * part : 3 * part + D] = y[2 * part :, 128 * side : 128 * side + 128]
                out[3 * part + D :] = jnp.concatenate([spare[2 * part :], jnp.zeros((D, 64), F32)], 1)


def pack(measured, mask, cut):
    shapes = []
    for d in range(cut.C):
        shapes += [jax.ShapeDtypeStruct((3 * cut.part + (2 * cut.D if d == 0 else 0), 128), F32)] * 2
    scratch = [
        pltpu.VMEM((cut.C, cut.ch, cut.S, cut.D, cut.W), F32),
        pltpu.VMEM(mask.shape, jnp.int32),
        pltpu.SemaphoreType.DMA((cut.C + 1,)),
    ]
    return call(functools.partial(pack_kernel, cut), "pack", (measured, mask), shapes, scratch, far=(0, 1), space=HBM)


def fold_kernel(kernel, out):
    half = kernel.shape[2] // 2
    out[...] = jnp.concatenate([kernel[:, :, :half], kernel[:, :, half:]], -1)


def weights_kernel(C, *refs):
    folded, (single, double, kernel) = refs[:C], refs[C:]
    taps, _, coils, inputs = kernel.shape
    half = folded[0].shape[2]
    for d in range(C):
        start = pl.multiple_of(lax.bitwise_xor(lax.axis_index("coil"), d) * 2 * half, 2 * half)
        kernel[:, :, pl.ds(start, half)] = folded[d][..., :inputs]
        kernel[:, :, pl.ds(start + half, half)] = folded[d][..., inputs:]

    def parts(tap):
        re, im = kernel[tap, 0], kernel[tap, 1]
        return re[:, :coils], im[:, :coils], re[:, coils:], im[:, coils:]

    N = 4 * coils
    for t in range(taps):
        pr, pi, vr, vi = parts(t)
        qr, qi, ur, ui = parts(taps - 1 - t)
        block = jnp.concatenate(
            [
                jnp.concatenate([pr, -pi, vr, vi], 1),
                jnp.concatenate([pi, pr, vi, -vr], 1),
                jnp.concatenate([ur, ui, qr, -qi], 1),
                jnp.concatenate([ui, -ur, qi, qr], 1),
            ],
            0,
        ).T
        hi, lo = split(block)
        e, tap = t % 3, t // 3
        single[tap, :, e * N : (e + 1) * N] = hi
        double[tap, :, 2 * e * N : (2 * e + 1) * N] = hi
        double[tap, :, (2 * e + 1) * N : (2 * e + 2) * N] = lo


def build_weights(C, folded, coils):
    taps, parts, _, inputs = folded[0].shape
    N = 4 * coils
    shapes = [jax.ShapeDtypeStruct((9, N, 3 * N), BF16), jax.ShapeDtypeStruct((9, N, 6 * N), BF16)]
    scratch = [pltpu.VMEM((taps, parts, coils, inputs // 2), F32)]
    return call(functools.partial(weights_kernel, C), "weights", folded, shapes, scratch)


def middle_row(cut, x):
    return jnp.where(lax.axis_index("kx") == 0, x[cut.S - 1], x[0])


def points_kernel(cut, ready, *refs):
    C, D, H, S, half = cut.C, cut.D, cut.H, cut.S, cut.half
    msgs, (x, marks, middle, main, spare) = refs[: 2 * C], refs[2 * C :]
    part = cut.part
    for d in range(C):
        other = lax.bitwise_xor(lax.axis_index("coil"), d)
        for side in range(2):
            msg = msgs[2 * d + side]
            for ri in range(2):
                start = pl.multiple_of(((side * 2 + ri) * C + other) * part, part)
                main[pl.ds(start, part)] = msg[ri * part : (ri + 1) * part]
            start = pl.multiple_of((side * C + other) * part, part)
            spare[pl.ds(start, part)] = msg[2 * part : 3 * part]

    def spread(target, k, first, rest):
        for r in range(cut.base):
            target[r, pl.ds(k, H, stride=D)] = first[r * H : (r + 1) * H]
        for r in range(cut.base, S):
            target[r, pl.ds(k, H, stride=D)] = rest[(r - cut.base) * H : (r - cut.base + 1) * H]
        for r in range(S):
            place = cut.spare + 2 * r
            target[r, pl.ds(H * D + k, 2, stride=D)] = rest[place : place + 2]

    lane = lax.broadcasted_iota(jnp.int32, (128, cut.channels), 1)
    flags = [msgs[side][3 * part : 3 * part + 2 * D] for side in range(2)]
    flags = jnp.concatenate(flags + [jnp.zeros((128 - 4 * D, 128), F32)], 0).T
    for k in range(D):
        j = D - 1 - k
        mine = main[pl.ds(k, half, stride=D)]
        other = main[pl.ds(half * D + j, half, stride=D)]
        first = jnp.concatenate([mine, other], 0).T
        mine = spare[pl.ds(k, half // 2, stride=D)]
        other = spare[pl.ds(half // 2 * D + j, half // 2, stride=D)]
        rest = jnp.concatenate([mine[:, :64], mine[:, 64:], other[:, :64], other[:, 64:]], 0)
        rest = jnp.concatenate([rest, jnp.zeros_like(rest)], 1).T
        spread(x, k, first, rest)
        first = jnp.where(lane < half, flags[:, k : k + 1], flags[:, 2 * D + j : 2 * D + j + 1])
        rest = jnp.where(lane < half, flags[:, D + k : D + k + 1], flags[:, 3 * D + j : 3 * D + j + 1])
        spread(marks, k, first, rest)
    middle[...] = middle_row(cut, x)


def points(ready, msgs, cut):
    row = (cut.V * cut.D, cut.channels)
    window = jax.ShapeDtypeStruct((cut.S, *row), F32)
    return call(
        functools.partial(points_kernel, cut),
        "points",
        (ready, *msgs),
        [window, window, jax.ShapeDtypeStruct(row, F32)],
        [pltpu.VMEM((cut.channels * cut.D, 128), F32), pltpu.VMEM((cut.half * cut.D, 128), F32)],
        far=(0,),
    )


def beside(cut, middle):
    _, c, x = place()
    inner = c == cut.C - 1
    middle = middle[...]
    before = jnp.where(jnp.logical_and(inner, x == 1), middle, 0.0)
    after = jnp.where(jnp.logical_and(inner, x == 0), middle, 0.0)
    return before, after


def faces_kernel(cut, x, middle, face_a, face_b, edges):
    D, S, V = cut.D, cut.S, cut.V
    edges[0], edges[1] = beside(cut, middle)
    odd = lax.rem(lax.axis_index("kz"), 2) == 1
    for slot in range(cut.slots):
        if slot == 0:
            row = edges.at[0]
        elif slot == S + 1:
            row = edges.at[1]
        else:
            row = x.at[slot - 1]
        first, final = row[pl.ds(0, V, stride=D)], row[pl.ds(D - 1, V, stride=D)]
        face_a[slot * V : (slot + 1) * V] = jnp.where(odd, first, final)
        face_b[slot * V : (slot + 1) * V] = jnp.where(odd, final, first)


def faces(x, middle, cut):
    face = jax.ShapeDtypeStruct((cut.slots * cut.V, cut.channels), F32)
    scratch = [pltpu.VMEM((2, cut.V * cut.D, cut.channels), F32)]
    return call(functools.partial(faces_kernel, cut), "faces", (x, middle), [face, face], scratch)


def multiply(hi, lo, single, double):
    N = single.shape[-1]
    groups = double.shape[-1] // (2 * 128)
    y, z = dot(hi, double), dot(lo, single)
    N = N // groups
    return [
        y[:, 2 * e * N : (2 * e + 1) * N] + y[:, (2 * e + 1) * N : (2 * e + 2) * N] + z[:, e * N : (e + 1) * N]
        for e in range(groups)
    ]


def inside_kernel(cut, last, x, middle, single, double, out, hi, lo):
    D, S = cut.D, cut.S
    count, L, channels = out.shape
    gap = jnp.zeros((D, channels), F32)
    before, after = beside(cut, middle)
    for slot in range(cut.slots):
        row = before if slot == 0 else after if slot == S + 1 else x[slot - 1]
        high = row.astype(BF16).astype(F32)
        for ref, value in ((hi, high), (lo, row - high)):
            ref[0, slot] = jnp.concatenate([gap, value[:-D]], 0).astype(BF16)
            ref[1, slot] = value.astype(BF16)
            ref[2, slot] = jnp.concatenate([value[D:], gap], 0).astype(BF16)
    first, _ = cut.range_of(last)

    def window(ref):
        return jnp.concatenate(
            [
                jnp.concatenate([ref[b, first + i + a, :L] for i in range(count)], 0)
                for a in range(3)
                for b in range(3)
            ],
            1,
        )

    K = 9 * channels
    y = multiply(window(hi), window(lo), single[...].reshape(K, -1), double[...].reshape(K, -1))
    rows = lax.broadcasted_iota(jnp.int32, (count * L, channels), 0) % D
    later = jnp.where(rows == 0, 0.0, pltpu.roll(y[0], 1, 0))
    sooner = jnp.where(rows == D - 1, 0.0, pltpu.roll(y[2], count * L - 1, 0))
    out[...] = (y[1] + later + sooner).reshape(count, L, channels)


def inside(x, middle, weights, cut, last):
    count = cut.range_of(last)[1]
    L = (cut.H if last else cut.V) * cut.D
    out = jax.ShapeDtypeStruct((count, L, cut.channels), F32)
    scratch = [pltpu.VMEM((3, cut.slots, cut.V * cut.D, cut.channels), BF16)] * 2
    return call(functools.partial(inside_kernel, cut, last), "inside", (x, middle, *weights), [out], scratch)[0]


def add_planes(cut, last, target, offset, count, got_a, got_b, single, double, planes):
    D, V, pitch = cut.D, cut.V, cut.pitch
    z, Z = lax.axis_index("kz"), lax.axis_size("kz")
    odd = lax.rem(z, 2) == 1
    ends = jnp.logical_or(z == 0, z == Z - 1)
    first, _ = cut.range_of(last)
    height = -(-count * pitch // 16) * 16
    width = cut.H if last else V
    N, K = cut.channels, 9 * cut.channels
    got_a, got_b = got_a[...], jnp.where(ends, 0.0, got_b[...])
    for e, k, plane in ((0, 0, jnp.where(odd, got_a, got_b)), (2, D - 1, jnp.where(odd, got_b, got_a))):
        planes[...] = jnp.zeros_like(planes)
        for slot in range(cut.slots):
            column = plane[slot * V : (slot + 1) * V]
            for b in range(3):
                place = 8 + slot * pitch + 1 - b
                planes[b, place : place + V] = column
        parts = [
            split(planes[b, pl.ds(pl.multiple_of(8 + (first + a) * pitch, 8), height)])
            for a in range(3)
            for b in range(3)
        ]
        hi, lo = (jnp.concatenate([part[i] for part in parts], 1) for i in range(2))
        one = single[:, :, e * N : (e + 1) * N].reshape(K, N)
        two = double[:, :, 2 * e * N : (2 * e + 2) * N].reshape(K, 2 * N)
        (y,) = multiply(hi, lo, one, two)
        for i in range(count):
            target[offset + i, pl.ds(k, width, stride=D)] += y[i * pitch : i * pitch + width]


def planes_scratch(cut):
    return pltpu.VMEM((3, 8 + cut.slots * cut.pitch + 16, cut.channels), F32)


def middle_kernel(cut, x, marks, main, got_a, got_b, single, double, out, middle, planes):
    first, count = cut.range_of(False)
    out[...] = jnp.zeros_like(out)
    for i in range(count):
        out[first + i] = main[i]
    add_planes(cut, False, out, first, count, got_a, got_b, single, double, planes)
    out[...] = jnp.where(marks[...] > 0.5, x[...], out[...])
    middle[...] = middle_row(cut, out)


def last_kernel(cut, main, got_a, got_b, single, double, *rest):
    C, D, H, G, half = cut.C, cut.D, cut.H, cut.G, cut.half
    outs, (y, stage, planes) = rest[: 2 * C], rest[2 * C :]
    y[...] = main[...]
    add_planes(cut, True, y, 0, G, got_a, got_b, single, double, planes)
    flip = reversal(G * H)
    for k in range(D):
        rows = y[:, pl.ds(k, H, stride=D)].reshape(G * H, 2 * half).T
        stage[pl.ds(k, half, stride=D)] = rows[:half]
        hi, lo = split(rows[half:])
        stage[pl.ds(half * D + D - 1 - k, half, stride=D)] = dot(hi, flip) + dot(lo, flip)
    for d in range(C):
        for side in range(2):
            for ri in range(2):
                start = ((side * 2 + ri) * C + lax.bitwise_xor(lax.axis_index("coil"), d)) * cut.part
                start = pl.multiple_of(start, cut.part)
                outs[2 * d + side][ri * cut.part : (ri + 1) * cut.part] = stage[pl.ds(start, cut.part)]


def unpack_kernel(cut, d, measured, mask, own, mirrored, *refs):
    out, rows, sem = refs[-3:]
    ch, D, G, H = cut.ch, cut.D, cut.G, cut.H
    start = cut.piece(d) * G
    own, mirrored = (msg[...].reshape(ch, D, G * H) for msg in (own, mirrored))
    for j in range(G):
        sampled = (mask[start + j] == 1)[None]
        value = jnp.concatenate([msg[:, :, j * H : (j + 1) * H] for msg in (own, mirrored)], -1)
        rows[:, j] = jnp.where(sampled, measured[:, start + j], value)
    copy = pltpu.make_async_copy(rows, out.at[:, pl.ds(start, G)], sem)
    copy.start()
    copy.wait()


def unpack(d, measured, mask, msgs, cut, into=None):
    args = (measured, mask, *msgs) + (() if into is None else (into,))
    (out,) = call(
        functools.partial(unpack_kernel, cut, d),
        "unpack",
        args,
        [jax.ShapeDtypeStruct(measured.shape, F32)],
        [pltpu.VMEM((cut.ch, cut.G, cut.D, cut.W), F32), pltpu.SemaphoreType.DMA],
        far=() if into is None else (len(args) - 1,),
        out=ANY,
        input_output_aliases={} if into is None else {len(args) - 1: 0},
    )
    return out


def on_device(measured, mask, kernel):
    Z, C, X = (lax.axis_size(axis) for axis in AXES)
    every = [(z, c, x) for z in range(Z) for c in range(C) for x in range(X)]

    def index(z, c, x):
        return (z * C + c) * X + x

    def send(array, target):
        return lax.ppermute(array, AXES, [(index(*p), index(*target(*p))) for p in every])

    def exchange(msgs):
        got = list(msgs)
        for d in range(C):
            got[2 * d + 1] = send(msgs[2 * d + 1], lambda z, c, x: (Z - 1 - z, c ^ d, X - 1 - x))
        for d in range(1, C):
            got[2 * d] = send(msgs[2 * d], lambda z, c, x: (z, c ^ d, x))
        return got

    def plane_a(z, c, x):
        return (z ^ 1, c, x)

    def plane_b(z, c, x):
        other = z + 1 if z % 2 else z - 1
        return (other, c, x) if 0 <= other < Z else (z, c, X - 1 - x)

    def core(z, c, x):
        return (z, c, X - 1 - x)

    parts, coils, rows, D, W = measured.shape
    cut = Cut(rows, D, W, C, 2 * parts * coils * C)
    flat = measured.reshape(parts * coils, rows, D, W)
    taps, _, _, inputs = kernel.shape
    msgs = pack(flat, mask, cut)
    kernel, *msgs = lax.optimization_barrier((kernel, *msgs))
    msgs = exchange(msgs)
    (folded,) = call(
        fold_kernel, "fold", (kernel,), [jax.ShapeDtypeStruct((taps, parts, coils // 2, 2 * inputs), F32)]
    )
    folded = [folded] + [send(folded, lambda z, c, x: (z, c ^ d, x)) for d in range(1, C)]
    weights = build_weights(C, folded, coils * C)
    state, marks, row = points(weights[0], msgs, cut)
    for step in range(ITERS):
        last = step == ITERS - 1
        row = send(row, core)
        face_a, face_b = faces(state, row, cut)
        got_a, got_b = send(face_a, plane_a), send(face_b, plane_b)
        main = inside(state, row, weights, cut, last)
        if not last:
            state, row = call(
                functools.partial(middle_kernel, cut),
                "middle",
                (state, marks, main, got_a, got_b, *weights),
                [jax.ShapeDtypeStruct(state.shape, F32), jax.ShapeDtypeStruct(row.shape, F32)],
                [planes_scratch(cut)],
            )
    message = jax.ShapeDtypeStruct((cut.ch * D, cut.G * cut.H), F32)
    msgs = call(
        functools.partial(last_kernel, cut),
        "last",
        (main, got_a, got_b, *weights),
        [message] * (2 * C),
        [pltpu.VMEM(main.shape, F32), pltpu.VMEM((cut.channels * D, cut.G * cut.H), F32), planes_scratch(cut)],
    )
    msgs = exchange(msgs)
    out = None
    for d in range(C):
        out = unpack(d, flat, mask, msgs[2 * d : 2 * d + 2], cut, out)
    return out.reshape(measured.shape)


def solution(mesh):
    placed = (
        P(None, ("grp", "coil"), "kx", "kz", None),
        P(("grp", "kx"), "kz", None),
        P(None, None, "coil", None),
    )
    return jax.shard_map(
        on_device,
        mesh=mesh,
        in_specs=placed,
        out_specs=P(None, ("grp", "coil"), "kx", "kz", None),
        check_vma=False,
    )
```

```python
import functools

import jax
import jax.numpy as jnp
from jax import lax
from jax.experimental import pallas as pl
from jax.experimental.pallas import tpu as pltpu
from jax.sharding import PartitionSpec as P

ITERS = 2
PACK = 56 << 20
AXES = ("kz", "coil", "kx")
F32 = jnp.float32
BF16 = jnp.bfloat16
ANY = pl.BlockSpec(memory_space=pl.ANY)
HBM = pl.BlockSpec(memory_space=pltpu.HBM)
VMEM = pl.BlockSpec(memory_space=pltpu.VMEM)


def call(body, name, args, shapes, scratch=(), far=(), space=ANY, out=VMEM, limit=48 << 20, **options):
    return pl.pallas_call(
        body,
        out_shape=shapes,
        in_specs=[space if i in far else VMEM for i in range(len(args))],
        out_specs=[out] * len(shapes),
        scratch_shapes=list(scratch),
        compiler_params=pltpu.CompilerParams(vmem_limit_bytes=limit),
        name=name,
        **options,
    )(*args)


def split(x):
    hi = x.astype(BF16)
    return hi, (x - hi.astype(F32)).astype(BF16)


def reversal(n):
    row = lax.broadcasted_iota(jnp.int32, (n, n), 0)
    column = lax.broadcasted_iota(jnp.int32, (n, n), 1)
    return jnp.where(row + column == n - 1, 1.0, 0.0).astype(BF16)


def dot(a, b):
    return jnp.dot(a, b, preferred_element_type=F32)


class Cut:
    def __init__(self, rows, D, W, C, channels):
        self.rows, self.D, self.W, self.C = rows, D, W, C
        self.channels = channels
        self.half = channels // 2
        self.ch = self.half // C
        self.G = rows // C
        self.S = min(rows, self.G + (2 if C == 2 else 4))
        self.H = W // 2
        self.V = self.H + 2
        self.base = 128 // self.H
        self.spare = (self.S - self.base) * self.H
        self.part = self.ch // 2 * D
        self.used = self.spare + 2 * self.S
        self.group = self.ch * D // 16
        self.folds = -(-16 * self.used // 128)
        self.length = 2 * self.part + self.folds * self.group
        self.slots = self.S + 2
        self.pitch = -(-(self.V + 1) // 8) * 8

    def piece(self, d=0):
        c, x = lax.bitwise_xor(lax.axis_index("coil"), d), lax.axis_index("kx")
        return jnp.where(x == 0, c, self.C - 1 - c)

    def start(self, d=0):
        return jnp.clip(self.G * self.piece(d) - 2, 0, self.rows - self.S)

    def range_of(self, last):
        own = self.G * self.piece() - self.start()
        if last:
            return own, self.G
        count = min(self.S, self.G + (1 if self.C == 2 else 2))
        return jnp.clip(own - 1, 0, self.S - count), count


def place():
    return tuple(lax.axis_index(axis) for axis in AXES)


def arrangement(cut):
    S, H, W = cut.S, cut.H, cut.W
    shift = H.bit_length() - 1
    j = lax.broadcasted_iota(jnp.int32, (1, 384), 1)
    own = j - jnp.where(j >= 320, 320, jnp.where(j >= 256, 256, jnp.where(j >= 128, 128, 0)))
    spare = j >= 256
    row = lax.shift_right_logical(own, shift)
    main = row * W + lax.bitwise_and(own, H - 1)
    rest = own - cut.spare
    edge = lax.shift_right_logical(rest, 1) * W + H + lax.bitwise_and(rest, 1)
    source = jnp.where(spare, jnp.where(own < cut.spare, main + cut.base * W, edge), main)
    mirrored = jnp.logical_or(jnp.logical_and(j >= 128, j < 256), j >= 320)
    source = jnp.where(mirrored, S * W - 1 - source, source)
    source = jnp.where(jnp.logical_and(spare, rest >= 2 * S), -1, source)
    lane = lax.broadcasted_iota(jnp.int32, (S * W, 384), 0)
    return jnp.where(lane == source, 1.0, 0.0).astype(BF16)


def pack_kernel(cut, d, measured, mask, *refs):
    S, ch, D, W, part = cut.S, cut.ch, cut.D, cut.W, cut.part
    outs, (rows, marks, sems) = refs[:2], refs[2:]
    start = cut.start(d)
    copies = [pltpu.make_async_copy(mask.at[pl.ds(start, S)], marks, sems.at[0])]
    copies.append(pltpu.make_async_copy(measured.at[:, pl.ds(start, S)], rows, sems.at[1]))
    for copy in copies:
        copy.start()
    order = arrangement(cut)
    for copy in copies:
        copy.wait()
    sampled = [marks[j] == 1 for j in range(S)]
    kept = [jnp.where(sampled[j][None], rows[:, j], 0.0) for j in range(S)]
    kept = jnp.concatenate(kept, -1).reshape(ch * D, S * W)
    if d == 0:
        kept = jnp.concatenate([kept, jnp.concatenate([jnp.where(s, 1.0, 0.0) for s in sampled], -1)], 0)
    hi, lo = split(kept)
    y = dot(hi, order) + dot(lo, order)
    for side in (1, 0):
        out = outs[side]
        out[: 2 * part] = y[: 2 * part, 128 * side : 128 * side + 128]
        spare = y[:, 256 + 64 * side : 320 + 64 * side]
        group = cut.group
        folded = [spare[i * group : (i + 1) * group, : cut.used] for i in range(16)]
        if cut.folds * 128 > 16 * cut.used:
            folded.append(jnp.zeros((group, cut.folds * 128 - 16 * cut.used), F32))
        folded = jnp.concatenate(folded, 1)
        for i in range(cut.folds):
            place = 2 * part + i * group
            out[place : place + group] = folded[:, i * 128 : (i + 1) * 128]
        if d == 0:
            out[cut.length : cut.length + D] = y[2 * part :, 128 * side : 128 * side + 128]
            out[cut.length + D :] = jnp.concatenate([spare[2 * part :], jnp.zeros((D, 64), F32)], 1)


def pack(d, measured, mask, cut):
    shapes = [jax.ShapeDtypeStruct((cut.length + (0 if d else 2 * cut.D), 128), F32)] * 2
    scratch = [
        pltpu.VMEM((cut.ch, cut.S, cut.D, cut.W), F32),
        pltpu.VMEM((cut.S, cut.D, cut.W), jnp.int32),
        pltpu.SemaphoreType.DMA((2,)),
    ]
    body = functools.partial(pack_kernel, cut, d)
    return call(body, "pack", (measured, mask), shapes, scratch, far=(0, 1), space=HBM, limit=PACK)


def fold_kernel(kernel, out):
    count = out.shape[0]
    half = kernel.shape[1] // 2
    some = kernel[pl.ds(lax.axis_index("kx") * count, count)]
    out[...] = jnp.concatenate([some[:, :half], some[:, half:]], -1)


def fold(kernel):
    count, coils, inputs = kernel.shape
    shape = jax.ShapeDtypeStruct((count // 2, coils // 2, 2 * inputs), F32)
    return call(fold_kernel, "fold", (kernel,), [shape])[0]


def weights_kernel(cut, own, *refs):
    folded, (single, double, kernel) = refs[:-3], refs[-3:]
    count, coils, inputs = kernel.shape
    local = coils // cut.C
    c, x = lax.axis_index("coil"), lax.axis_index("kx")
    kernel[:, pl.ds(pl.multiple_of(c * local, local), local)] = own[...]
    for i, half in enumerate(folded):
        d, other = i // 2 + 1, i % 2
        place = pl.multiple_of(lax.bitwise_xor(c, d) * local, local)
        taps = pl.ds(lax.bitwise_xor(x, other) * (count // 2), count // 2)
        kernel[taps, pl.ds(place, local // 2)] = half[..., :inputs]
        kernel[taps, pl.ds(place + local // 2, local // 2)] = half[..., inputs:]

    def parts(tap):
        re, im = kernel[2 * tap], kernel[2 * tap + 1]
        return re[:, :coils], im[:, :coils], re[:, coils:], im[:, coils:]

    N = 4 * coils
    taps = count // 2
    for t in range(taps):
        pr, pi, vr, vi = parts(t)
        qr, qi, ur, ui = parts(taps - 1 - t)
        block = jnp.concatenate(
            [
                jnp.concatenate([pr, -pi, vr, vi], 1),
                jnp.concatenate([pi, pr, vi, -vr], 1),
                jnp.concatenate([ur, ui, qr, -qi], 1),
                jnp.concatenate([ui, -ur, qi, qr], 1),
            ],
            0,
        ).T
        hi, lo = split(block)
        e, tap = t % 3, t // 3
        single[tap, :, e * N : (e + 1) * N] = hi
        double[tap, :, 2 * e * N : (2 * e + 1) * N] = hi
        double[tap, :, (2 * e + 1) * N : (2 * e + 2) * N] = lo


def build_weights(kernel, folded, cut):
    count, coils, inputs = kernel.shape
    N = cut.channels
    shapes = [jax.ShapeDtypeStruct((9, N, 3 * N), BF16), jax.ShapeDtypeStruct((9, N, 6 * N), BF16)]
    scratch = [pltpu.VMEM((count, coils * cut.C, inputs), F32)]
    return call(functools.partial(weights_kernel, cut), "weights", (kernel, *folded), shapes, scratch)


def middle_row(cut, x):
    return jnp.where(lax.axis_index("kx") == 0, x[cut.S - 1], x[0])


def points_kernel(cut, ready, *refs):
    C, D, H, S, half = cut.C, cut.D, cut.H, cut.S, cut.half
    msgs, (x, marks, middle, main, spare) = refs[: 2 * C], refs[2 * C :]
    part = cut.part
    for d in range(C):
        other = lax.bitwise_xor(lax.axis_index("coil"), d)
        for side in range(2):
            msg = msgs[2 * d + side]
            for ri in range(2):
                start = pl.multiple_of(((side * 2 + ri) * C + other) * part, part)
                main[pl.ds(start, part)] = msg[ri * part : (ri + 1) * part]
            folded = msg[2 * part : cut.length].reshape(cut.folds, cut.group, 128)
            folded = jnp.concatenate([folded[i] for i in range(cut.folds)], 1)
            for i in range(16):
                ri, rest = i // 8, i % 8 * cut.group
                start = pl.multiple_of(((side * 2 + ri) * C + other) * part + rest, cut.group)
                spare[pl.ds(start, cut.group), : cut.used] = folded[:, i * cut.used : (i + 1) * cut.used]

    def spread(target, k, first, rest):
        for r in range(cut.base):
            target[r, pl.ds(k, H, stride=D)] = first[r * H : (r + 1) * H]
        for r in range(cut.base, S):
            target[r, pl.ds(k, H, stride=D)] = rest[(r - cut.base) * H : (r - cut.base + 1) * H]
        for r in range(S):
            place = cut.spare + 2 * r
            target[r, pl.ds(H * D + k, 2, stride=D)] = rest[place : place + 2]

    lane = lax.broadcasted_iota(jnp.int32, (128, cut.channels), 1)
    flags = [msgs[side][cut.length : cut.length + 2 * D] for side in range(2)]
    flags = jnp.concatenate(flags + [jnp.zeros((128 - 4 * D, 128), F32)], 0).T
    for k in range(D):
        j = D - 1 - k
        mine = main[pl.ds(k, half, stride=D)]
        other = main[pl.ds(half * D + j, half, stride=D)]
        first = jnp.concatenate([mine, other], 0).T
        mine = spare[pl.ds(k, half, stride=D)]
        other = spare[pl.ds(half * D + j, half, stride=D)]
        rest = jnp.concatenate([mine, other], 0).T
        spread(x, k, first, rest)
        first = jnp.where(lane < half, flags[:, k : k + 1], flags[:, 2 * D + j : 2 * D + j + 1])
        rest = jnp.where(lane < half, flags[:, D + k : D + k + 1], flags[:, 3 * D + j : 3 * D + j + 1])
        spread(marks, k, first, rest)
    middle[...] = middle_row(cut, x)


def points(ready, msgs, cut):
    row = (cut.V * cut.D, cut.channels)
    window = jax.ShapeDtypeStruct((cut.S, *row), F32)
    return call(
        functools.partial(points_kernel, cut),
        "points",
        (ready, *msgs),
        [window, window, jax.ShapeDtypeStruct(row, F32)],
        [pltpu.VMEM((cut.channels * cut.D, 128), F32)] * 2,
        far=(0,),
    )


def beside(cut, middle):
    _, c, x = place()
    inner = c == cut.C - 1
    middle = middle[...]
    before = jnp.where(jnp.logical_and(inner, x == 1), middle, 0.0)
    after = jnp.where(jnp.logical_and(inner, x == 0), middle, 0.0)
    return before, after


def faces_kernel(cut, x, middle, face_a, face_b, edges):
    D, S, V = cut.D, cut.S, cut.V
    edges[0], edges[1] = beside(cut, middle)
    odd = lax.rem(lax.axis_index("kz"), 2) == 1
    for slot in range(cut.slots):
        if slot == 0:
            row = edges.at[0]
        elif slot == S + 1:
            row = edges.at[1]
        else:
            row = x.at[slot - 1]
        first, final = row[pl.ds(0, V, stride=D)], row[pl.ds(D - 1, V, stride=D)]
        face_a[slot * V : (slot + 1) * V] = jnp.where(odd, first, final)
        face_b[slot * V : (slot + 1) * V] = jnp.where(odd, final, first)


def faces(x, middle, cut):
    face = jax.ShapeDtypeStruct((cut.slots * cut.V, cut.channels), F32)
    scratch = [pltpu.VMEM((2, cut.V * cut.D, cut.channels), F32)]
    return call(functools.partial(faces_kernel, cut), "faces", (x, middle), [face, face], scratch)


def multiply(hi, lo, single, double):
    N = single.shape[-1]
    groups = double.shape[-1] // (2 * 128)
    y, z = dot(hi, double), dot(lo, single)
    N = N // groups
    return [
        y[:, 2 * e * N : (2 * e + 1) * N] + y[:, (2 * e + 1) * N : (2 * e + 2) * N] + z[:, e * N : (e + 1) * N]
        for e in range(groups)
    ]


def inside_kernel(cut, last, x, middle, single, double, out, hi, lo):
    D, S = cut.D, cut.S
    count, L, channels = out.shape
    gap = jnp.zeros((D, channels), F32)
    before, after = beside(cut, middle)
    for slot in range(cut.slots):
        row = before if slot == 0 else after if slot == S + 1 else x[slot - 1]
        high = row.astype(BF16).astype(F32)
        for ref, value in ((hi, high), (lo, row - high)):
            ref[0, slot] = jnp.concatenate([gap, value[:-D]], 0).astype(BF16)
            ref[1, slot] = value.astype(BF16)
            ref[2, slot] = jnp.concatenate([value[D:], gap], 0).astype(BF16)
    first, _ = cut.range_of(last)

    def window(ref):
        return jnp.concatenate(
            [
                jnp.concatenate([ref[b, first + i + a, :L] for i in range(count)], 0)
                for a in range(3)
                for b in range(3)
            ],
            1,
        )

    K = 9 * channels
    y = multiply(window(hi), window(lo), single[...].reshape(K, -1), double[...].reshape(K, -1))
    rows = lax.broadcasted_iota(jnp.int32, (count * L, channels), 0) % D
    later = jnp.where(rows == 0, 0.0, pltpu.roll(y[0], 1, 0))
    sooner = jnp.where(rows == D - 1, 0.0, pltpu.roll(y[2], count * L - 1, 0))
    out[...] = (y[1] + later + sooner).reshape(count, L, channels)


def inside(x, middle, weights, cut, last):
    count = cut.range_of(last)[1]
    L = (cut.H if last else cut.V) * cut.D
    out = jax.ShapeDtypeStruct((count, L, cut.channels), F32)
    scratch = [pltpu.VMEM((3, cut.slots, cut.V * cut.D, cut.channels), BF16)] * 2
    return call(functools.partial(inside_kernel, cut, last), "inside", (x, middle, *weights), [out], scratch)[0]


def add_planes(cut, last, target, offset, count, got_a, got_b, single, double, planes):
    D, V, pitch = cut.D, cut.V, cut.pitch
    z, Z = lax.axis_index("kz"), lax.axis_size("kz")
    odd = lax.rem(z, 2) == 1
    ends = jnp.logical_or(z == 0, z == Z - 1)
    first, _ = cut.range_of(last)
    height = -(-count * pitch // 16) * 16
    width = cut.H if last else V
    N, K = cut.channels, 9 * cut.channels
    got_a, got_b = got_a[...], jnp.where(ends, 0.0, got_b[...])
    for e, k, plane in ((0, 0, jnp.where(odd, got_a, got_b)), (2, D - 1, jnp.where(odd, got_b, got_a))):
        planes[...] = jnp.zeros_like(planes)
        for slot in range(cut.slots):
            column = plane[slot * V : (slot + 1) * V]
            for b in range(3):
                place = 8 + slot * pitch + 1 - b
                planes[b, place : place + V] = column
        parts = [
            split(planes[b, pl.ds(pl.multiple_of(8 + (first + a) * pitch, 8), height)])
            for a in range(3)
            for b in range(3)
        ]
        hi, lo = (jnp.concatenate([part[i] for part in parts], 1) for i in range(2))
        one = single[:, :, e * N : (e + 1) * N].reshape(K, N)
        two = double[:, :, 2 * e * N : (2 * e + 2) * N].reshape(K, 2 * N)
        (y,) = multiply(hi, lo, one, two)
        for i in range(count):
            target[offset + i, pl.ds(k, width, stride=D)] += y[i * pitch : i * pitch + width]


def planes_scratch(cut):
    return pltpu.VMEM((3, 8 + cut.slots * cut.pitch + 16, cut.channels), F32)


def middle_kernel(cut, x, marks, main, got_a, got_b, single, double, out, middle, planes):
    first, count = cut.range_of(False)
    out[...] = jnp.zeros_like(out)
    for i in range(count):
        out[first + i] = main[i]
    add_planes(cut, False, out, first, count, got_a, got_b, single, double, planes)
    out[...] = jnp.where(marks[...] > 0.5, x[...], out[...])
    middle[...] = middle_row(cut, out)


def last_kernel(cut, main, got_a, got_b, single, double, *rest):
    C, D, H, G, half = cut.C, cut.D, cut.H, cut.G, cut.half
    outs, (y, stage, planes) = rest[: 2 * C], rest[2 * C :]
    y[...] = main[...]
    add_planes(cut, True, y, 0, G, got_a, got_b, single, double, planes)
    flip = reversal(G * H)
    for k in range(D):
        rows = y[:, pl.ds(k, H, stride=D)].reshape(G * H, 2 * half).T
        stage[pl.ds(k, half, stride=D)] = rows[:half]
        hi, lo = split(rows[half:])
        stage[pl.ds(half * D + D - 1 - k, half, stride=D)] = dot(hi, flip) + dot(lo, flip)
    for d in range(C):
        for side in range(2):
            for ri in range(2):
                start = ((side * 2 + ri) * C + lax.bitwise_xor(lax.axis_index("coil"), d)) * cut.part
                start = pl.multiple_of(start, cut.part)
                outs[2 * d + side][ri * cut.part : (ri + 1) * cut.part] = stage[pl.ds(start, cut.part)]


def unpack_kernel(cut, d, measured, mask, own, mirrored, *refs):
    out, rows, sems = refs[-3:]
    ch, D, G, H = cut.ch, cut.D, cut.G, cut.H
    start = cut.piece(d) * G
    own, mirrored = (msg[...].reshape(ch, D, G * H) for msg in (own, mirrored))
    copies = []
    for j in range(G):
        sampled = (mask[start + j] == 1)[None]
        value = jnp.concatenate([msg[:, :, j * H : (j + 1) * H] for msg in (own, mirrored)], -1)
        rows[:, j] = jnp.where(sampled, measured[:, start + j], value)
        if j % 2:
            some = pl.ds(j - 1, 2)
            copy = pltpu.make_async_copy(rows.at[:, some], out.at[:, pl.ds(start + j - 1, 2)], sems.at[j // 2])
            copy.start()
            copies.append(copy)
    for copy in copies:
        copy.wait()


def unpack(d, measured, mask, msgs, cut, into=None):
    args = (measured, mask, *msgs) + (() if into is None else (into,))
    (out,) = call(
        functools.partial(unpack_kernel, cut, d),
        "unpack",
        args,
        [jax.ShapeDtypeStruct(measured.shape, F32)],
        [pltpu.VMEM((cut.ch, cut.G, cut.D, cut.W), F32), pltpu.SemaphoreType.DMA((cut.G // 2,))],
        far=() if into is None else (len(args) - 1,),
        out=ANY,
        input_output_aliases={} if into is None else {len(args) - 1: 0},
    )
    return out


def on_device(measured, mask, kernel):
    Z, C, X = (lax.axis_size(axis) for axis in AXES)
    every = [(z, c, x) for z in range(Z) for c in range(C) for x in range(X)]

    def index(z, c, x):
        return (z * C + c) * X + x

    def send(array, target):
        return lax.ppermute(array, AXES, [(index(*p), index(*target(*p))) for p in every])

    def exchange(msgs):
        got = list(msgs)
        for d in range(C):
            got[2 * d + 1] = send(msgs[2 * d + 1], lambda z, c, x: (Z - 1 - z, c ^ d, X - 1 - x))
        for d in range(1, C):
            got[2 * d] = send(msgs[2 * d], lambda z, c, x: (z, c ^ d, x))
        return got

    def plane_a(z, c, x):
        return (z ^ 1, c, x)

    def plane_b(z, c, x):
        other = z + 1 if z % 2 else z - 1
        return (other, c, x) if 0 <= other < Z else (z, c, X - 1 - x)

    def core(z, c, x):
        return (z, c, X - 1 - x)

    parts, coils, rows, D, W = measured.shape
    cut = Cut(rows, D, W, C, 2 * parts * coils * C)
    flat = measured.reshape(parts * coils, rows, D, W)
    kernel = kernel.reshape(-1, *kernel.shape[2:])
    msgs = pack(0, flat, mask, cut)
    for d in range(1, C):
        kernel, mask, *msgs = lax.optimization_barrier((kernel, mask, *msgs))
        msgs = [*msgs, *pack(d, flat, mask, cut)]
    msgs = exchange(msgs)
    folded = []
    for d in range(1, C):
        half = send(fold(kernel), lambda z, c, x: (z, c ^ d, x))
        folded += [half, send(half, core)]
    weights = build_weights(kernel, folded, cut)
    state, marks, row = points(weights[0], msgs, cut)
    for step in range(ITERS):
        last = step == ITERS - 1
        row = send(row, core)
        face_a, face_b = faces(state, row, cut)
        got_a, got_b = send(face_a, plane_a), send(face_b, plane_b)
        main = inside(state, row, weights, cut, last)
        if not last:
            state, row = call(
                functools.partial(middle_kernel, cut),
                "middle",
                (state, marks, main, got_a, got_b, *weights),
                [jax.ShapeDtypeStruct(state.shape, F32), jax.ShapeDtypeStruct(row.shape, F32)],
                [planes_scratch(cut)],
            )
    message = jax.ShapeDtypeStruct((cut.ch * D, cut.G * cut.H), F32)
    msgs = call(
        functools.partial(last_kernel, cut),
        "last",
        (main, got_a, got_b, *weights),
        [message] * (2 * C),
        [pltpu.VMEM(main.shape, F32), pltpu.VMEM((cut.channels * D, cut.G * cut.H), F32), planes_scratch(cut)],
    )
    msgs = exchange(msgs)
    out = None
    for d in range(C):
        out = unpack(d, flat, mask, msgs[2 * d : 2 * d + 2], cut, out)
    return out.reshape(measured.shape)


def solution(mesh):
    placed = (
        P(None, ("grp", "coil"), "kx", "kz", None),
        P(("grp", "kx"), "kz", None),
        P(None, None, "coil", None),
    )
    return jax.shard_map(
        on_device,
        mesh=mesh,
        in_specs=placed,
        out_specs=P(None, ("grp", "coil"), "kx", "kz", None),
        check_vma=False,
    )
```

```python
import functools

import jax
import jax.numpy as jnp
from jax import lax
from jax.experimental import pallas as pl
from jax.experimental.pallas import tpu as pltpu
from jax.sharding import PartitionSpec as P

ITERS = 2
PACK = 56 << 20
LITTLE = pl.CostEstimate(flops=1000, bytes_accessed=1000, transcendentals=0)
AXES = ("kz", "coil", "kx")
F32 = jnp.float32
BF16 = jnp.bfloat16
ANY = pl.BlockSpec(memory_space=pl.ANY)
HBM = pl.BlockSpec(memory_space=pltpu.HBM)
VMEM = pl.BlockSpec(memory_space=pltpu.VMEM)


def call(body, name, args, shapes, scratch=(), far=(), space=ANY, out=VMEM, limit=48 << 20, cost=None, **options):
    return pl.pallas_call(
        body,
        out_shape=shapes,
        in_specs=[space if i in far else VMEM for i in range(len(args))],
        out_specs=[out] * len(shapes),
        scratch_shapes=list(scratch),
        compiler_params=pltpu.CompilerParams(vmem_limit_bytes=limit),
        cost_estimate=cost,
        name=name,
        **options,
    )(*args)


def split(x):
    hi = x.astype(BF16)
    return hi, (x - hi.astype(F32)).astype(BF16)


def reversal(n):
    row = lax.broadcasted_iota(jnp.int32, (n, n), 0)
    column = lax.broadcasted_iota(jnp.int32, (n, n), 1)
    return jnp.where(row + column == n - 1, 1.0, 0.0).astype(BF16)


def dot(a, b):
    return jnp.dot(a, b, preferred_element_type=F32)


class Cut:
    def __init__(self, rows, D, W, C, channels):
        self.rows, self.D, self.W, self.C = rows, D, W, C
        self.channels = channels
        self.half = channels // 2
        self.ch = self.half // C
        self.G = rows // C
        self.S = min(rows, self.G + (2 if C == 2 else 4))
        self.H = W // 2
        self.V = self.H + 2
        self.base = 128 // self.H
        self.spare = (self.S - self.base) * self.H
        self.part = self.ch // 2 * D
        self.used = self.spare + 2 * self.S
        self.group = self.ch * D // 16
        self.folds = -(-16 * self.used // 128)
        self.length = 2 * self.part + self.folds * self.group
        self.slots = self.S + 2
        self.pitch = -(-(self.V + 1) // 8) * 8

    def piece(self, d=0):
        c, x = lax.bitwise_xor(lax.axis_index("coil"), d), lax.axis_index("kx")
        return jnp.where(x == 0, c, self.C - 1 - c)

    def start(self, d=0):
        return jnp.clip(self.G * self.piece(d) - 2, 0, self.rows - self.S)

    def range_of(self, last):
        own = self.G * self.piece() - self.start()
        if last:
            return own, self.G
        count = min(self.S, self.G + (1 if self.C == 2 else 2))
        return jnp.clip(own - 1, 0, self.S - count), count


def place():
    return tuple(lax.axis_index(axis) for axis in AXES)


def arrangement(cut):
    S, H, W = cut.S, cut.H, cut.W
    shift = H.bit_length() - 1
    j = lax.broadcasted_iota(jnp.int32, (1, 384), 1)
    own = j - jnp.where(j >= 320, 320, jnp.where(j >= 256, 256, jnp.where(j >= 128, 128, 0)))
    spare = j >= 256
    row = lax.shift_right_logical(own, shift)
    main = row * W + lax.bitwise_and(own, H - 1)
    rest = own - cut.spare
    edge = lax.shift_right_logical(rest, 1) * W + H + lax.bitwise_and(rest, 1)
    source = jnp.where(spare, jnp.where(own < cut.spare, main + cut.base * W, edge), main)
    mirrored = jnp.logical_or(jnp.logical_and(j >= 128, j < 256), j >= 320)
    source = jnp.where(mirrored, S * W - 1 - source, source)
    source = jnp.where(jnp.logical_and(spare, rest >= 2 * S), -1, source)
    lane = lax.broadcasted_iota(jnp.int32, (S * W, 384), 0)
    return jnp.where(lane == source, 1.0, 0.0).astype(BF16)


def pack_kernel(cut, d, measured, mask, *refs):
    S, ch, D, W, part = cut.S, cut.ch, cut.D, cut.W, cut.part
    outs, (rows, marks, sems) = refs[:2], refs[2:]
    start = cut.start(d)
    copies = [pltpu.make_async_copy(mask.at[pl.ds(start, S)], marks, sems.at[0])]
    copies.append(pltpu.make_async_copy(measured.at[:, pl.ds(start, S)], rows, sems.at[1]))
    for copy in copies:
        copy.start()
    order = arrangement(cut)
    for copy in copies:
        copy.wait()
    sampled = [marks[j] == 1 for j in range(S)]
    kept = [jnp.where(sampled[j][None], rows[:, j], 0.0) for j in range(S)]
    kept = jnp.concatenate(kept, -1).reshape(ch * D, S * W)
    if d < 2:
        kept = jnp.concatenate([kept, jnp.concatenate([jnp.where(s, 1.0, 0.0) for s in sampled], -1)], 0)
    hi, lo = split(kept)
    y = dot(hi, order) + dot(lo, order)
    for side in (1, 0):
        out = outs[side]
        out[: 2 * part] = y[: 2 * part, 128 * side : 128 * side + 128]
        spare = y[:, 256 + 64 * side : 320 + 64 * side]
        group = cut.group
        folded = [spare[i * group : (i + 1) * group, : cut.used] for i in range(16)]
        if cut.folds * 128 > 16 * cut.used:
            folded.append(jnp.zeros((group, cut.folds * 128 - 16 * cut.used), F32))
        folded = jnp.concatenate(folded, 1)
        for i in range(cut.folds):
            place = 2 * part + i * group
            out[place : place + group] = folded[:, i * 128 : (i + 1) * 128]
        if d == side:
            out[cut.length : cut.length + D] = y[2 * part :, 128 * side : 128 * side + 128]
            out[cut.length + D :] = jnp.concatenate([spare[2 * part :], jnp.zeros((D, 64), F32)], 1)


def pack(d, measured, mask, cut):
    shapes = [jax.ShapeDtypeStruct((cut.length + (2 * cut.D if d == side else 0), 128), F32) for side in range(2)]
    scratch = [
        pltpu.VMEM((cut.ch, cut.S, cut.D, cut.W), F32),
        pltpu.VMEM((cut.S, cut.D, cut.W), jnp.int32),
        pltpu.SemaphoreType.DMA((2,)),
    ]
    body = functools.partial(pack_kernel, cut, d)
    return call(body, "pack", (measured, mask), shapes, scratch, far=(0, 1), space=HBM, limit=PACK)


def fold_kernel(kernel, out):
    count = out.shape[0]
    half = kernel.shape[1] // 2
    some = kernel[pl.ds(lax.axis_index("kx") * count, count)]
    out[...] = jnp.concatenate([some[:, :half], some[:, half:]], -1)


def fold(kernel):
    count, coils, inputs = kernel.shape
    shape = jax.ShapeDtypeStruct((count // 2, coils // 2, 2 * inputs), F32)
    return call(fold_kernel, "fold", (kernel,), [shape])[0]


def weights_kernel(cut, own, *refs):
    folded, (single, double, kernel) = refs[:-3], refs[-3:]
    count, coils, inputs = kernel.shape
    local = coils // cut.C
    c, x = lax.axis_index("coil"), lax.axis_index("kx")
    kernel[:, pl.ds(pl.multiple_of(c * local, local), local)] = own[...]
    for i, half in enumerate(folded):
        d, other = i // 2 + 1, i % 2
        place = pl.multiple_of(lax.bitwise_xor(c, d) * local, local)
        taps = pl.ds(lax.bitwise_xor(x, other) * (count // 2), count // 2)
        kernel[taps, pl.ds(place, local // 2)] = half[..., :inputs]
        kernel[taps, pl.ds(place + local // 2, local // 2)] = half[..., inputs:]

    def parts(tap):
        re, im = kernel[2 * tap], kernel[2 * tap + 1]
        return re[:, :coils], im[:, :coils], re[:, coils:], im[:, coils:]

    N = 4 * coils
    taps = count // 2
    for t in range(taps):
        pr, pi, vr, vi = parts(t)
        qr, qi, ur, ui = parts(taps - 1 - t)
        block = jnp.concatenate(
            [
                jnp.concatenate([pr, -pi, vr, vi], 1),
                jnp.concatenate([pi, pr, vi, -vr], 1),
                jnp.concatenate([ur, ui, qr, -qi], 1),
                jnp.concatenate([ui, -ur, qi, qr], 1),
            ],
            0,
        ).T
        hi, lo = split(block)
        e, tap = t % 3, t // 3
        single[tap, :, e * N : (e + 1) * N] = hi
        double[tap, :, 2 * e * N : (2 * e + 1) * N] = hi
        double[tap, :, (2 * e + 1) * N : (2 * e + 2) * N] = lo


def build_weights(kernel, folded, cut):
    count, coils, inputs = kernel.shape
    N = cut.channels
    shapes = [jax.ShapeDtypeStruct((9, N, 3 * N), BF16), jax.ShapeDtypeStruct((9, N, 6 * N), BF16)]
    scratch = [pltpu.VMEM((count, coils * cut.C, inputs), F32)]
    return call(functools.partial(weights_kernel, cut), "weights", (kernel, *folded), shapes, scratch, cost=LITTLE)


def middle_row(cut, x):
    return jnp.where(lax.axis_index("kx") == 0, x[cut.S - 1], x[0])


def spread(cut, target, k, first, rest):
    D, H, S = cut.D, cut.H, cut.S
    for r in range(cut.base):
        target[r, pl.ds(k, H, stride=D)] = first[r * H : (r + 1) * H]
    for r in range(cut.base, S):
        target[r, pl.ds(k, H, stride=D)] = rest[(r - cut.base) * H : (r - cut.base + 1) * H]
    for r in range(S):
        place = cut.spare + 2 * r
        target[r, pl.ds(H * D + k, 2, stride=D)] = rest[place : place + 2]


def assemble(cut, side, msgs, x, main, spare):
    D, half, part = cut.D, cut.half, cut.part
    for d, msg in enumerate(msgs):
        other = lax.bitwise_xor(lax.axis_index("coil"), d)
        folded = msg[2 * part : cut.length].reshape(cut.folds, cut.group, 128)
        folded = jnp.concatenate([folded[i] for i in range(cut.folds)], 1)
        for ri in range(2):
            start = pl.multiple_of((ri * cut.C + other) * part, part)
            main[pl.ds(start, part)] = msg[ri * part : (ri + 1) * part]
        for i in range(16):
            start = pl.multiple_of((i // 8 * cut.C + other) * part + i % 8 * cut.group, cut.group)
            spare[pl.ds(start, cut.group), : cut.used] = folded[:, i * cut.used : (i + 1) * cut.used]
    gap = jnp.zeros((half, 128), F32)
    for k in range(D):
        some = pl.ds(D - 1 - k if side else k, half, stride=D)
        blocks = [jnp.concatenate([gap, v] if side else [v, gap], 0).T for v in (main[some], spare[some])]
        spread(cut, x, k, *blocks)


def physical_kernel(cut, ready, *refs):
    msgs, (x, main, spare) = refs[: cut.C], refs[cut.C :]
    assemble(cut, 0, msgs, x, main, spare)


def mirrored_kernel(cut, physical, *refs):
    msgs, (x, middle, main, spare) = refs[: cut.C], refs[-4:]
    assemble(cut, 1, msgs, x, main, spare)
    x[...] = x[...] + physical[...]
    middle[...] = middle_row(cut, x)


def marks_kernel(cut, ready, own, other, marks):
    D, half = cut.D, cut.half
    lane = lax.broadcasted_iota(jnp.int32, (128, cut.channels), 1)
    flags = [msg[cut.length : cut.length + 2 * D] for msg in (own, other)]
    flags = jnp.concatenate(flags + [jnp.zeros((128 - 4 * D, 128), F32)], 0).T
    for k in range(D):
        j = D - 1 - k
        first = jnp.where(lane < half, flags[:, k : k + 1], flags[:, 2 * D + j : 2 * D + j + 1])
        rest = jnp.where(lane < half, flags[:, D + k : D + k + 1], flags[:, 3 * D + j : 3 * D + j + 1])
        spread(cut, marks, k, first, rest)


def points(cut, weights, msgs):
    row = (cut.V * cut.D, cut.channels)
    window = jax.ShapeDtypeStruct((cut.S, *row), F32)
    stages = [pltpu.VMEM((cut.half * cut.D, 128), F32)] * 2
    args = (weights[0], *msgs[0::2])
    (x,) = call(functools.partial(physical_kernel, cut), "physical", args, [window], stages, far=(0,), cost=LITTLE)
    added = inside_half(0, x, weights, cut)
    flags = (added, msgs[0], msgs[3])
    (marks,) = call(functools.partial(marks_kernel, cut), "marks", flags, [window], far=(0,), cost=LITTLE)
    args = (x, *msgs[1::2], added, marks)
    x, middle = call(
        functools.partial(mirrored_kernel, cut),
        "mirrored",
        args,
        [window, jax.ShapeDtypeStruct(row, F32)],
        stages,
        far=(len(args) - 2, len(args) - 1),
    )
    return x, marks, middle, added


def beside(cut, middle):
    _, c, x = place()
    inner = c == cut.C - 1
    middle = middle[...]
    before = jnp.where(jnp.logical_and(inner, x == 1), middle, 0.0)
    after = jnp.where(jnp.logical_and(inner, x == 0), middle, 0.0)
    return before, after


def faces_kernel(cut, x, middle, face_a, face_b, edges):
    D, S, V = cut.D, cut.S, cut.V
    edges[0], edges[1] = beside(cut, middle)
    odd = lax.rem(lax.axis_index("kz"), 2) == 1
    for slot in range(cut.slots):
        if slot == 0:
            row = edges.at[0]
        elif slot == S + 1:
            row = edges.at[1]
        else:
            row = x.at[slot - 1]
        first, final = row[pl.ds(0, V, stride=D)], row[pl.ds(D - 1, V, stride=D)]
        face_a[slot * V : (slot + 1) * V] = jnp.where(odd, first, final)
        face_b[slot * V : (slot + 1) * V] = jnp.where(odd, final, first)


def faces(x, middle, cut):
    face = jax.ShapeDtypeStruct((cut.slots * cut.V, cut.channels), F32)
    scratch = [pltpu.VMEM((2, cut.V * cut.D, cut.channels), F32)]
    return call(functools.partial(faces_kernel, cut), "faces", (x, middle), [face, face], scratch)


def multiply(hi, lo, single, double):
    N = single.shape[-1]
    groups = double.shape[-1] // (2 * 128)
    y, z = dot(hi, double), dot(lo, single)
    N = N // groups
    return [
        y[:, 2 * e * N : (2 * e + 1) * N] + y[:, (2 * e + 1) * N : (2 * e + 2) * N] + z[:, e * N : (e + 1) * N]
        for e in range(groups)
    ]


def shifted(y, D):
    M = y[0].shape[0]
    rows = lax.broadcasted_iota(jnp.int32, y[0].shape, 0) % D
    later = jnp.where(rows == 0, 0.0, pltpu.roll(y[0], 1, 0))
    sooner = jnp.where(rows == D - 1, 0.0, pltpu.roll(y[2], M - 1, 0))
    return y[1] + later + sooner


def inside_kernel(cut, last, x, middle, single, double, out, hi, lo):
    D, S = cut.D, cut.S
    count, L, channels = out.shape
    gap = jnp.zeros((D, channels), F32)
    before, after = beside(cut, middle)
    for slot in range(cut.slots):
        row = before if slot == 0 else after if slot == S + 1 else x[slot - 1]
        high = row.astype(BF16).astype(F32)
        for ref, value in ((hi, high), (lo, row - high)):
            ref[0, slot] = jnp.concatenate([gap, value[:-D]], 0).astype(BF16)
            ref[1, slot] = value.astype(BF16)
            ref[2, slot] = jnp.concatenate([value[D:], gap], 0).astype(BF16)
    first, _ = cut.range_of(last)

    def window(ref):
        return jnp.concatenate(
            [
                jnp.concatenate([ref[b, first + i + a, :L] for i in range(count)], 0)
                for a in range(3)
                for b in range(3)
            ],
            1,
        )

    K = 9 * channels
    y = multiply(window(hi), window(lo), single[...].reshape(K, -1), double[...].reshape(K, -1))
    out[...] = shifted(y, D).reshape(count, L, channels)


def inside(x, middle, weights, cut, last):
    count = cut.range_of(last)[1]
    L = (cut.H if last else cut.V) * cut.D
    out = jax.ShapeDtypeStruct((count, L, cut.channels), F32)
    scratch = [pltpu.VMEM((3, cut.slots, cut.V * cut.D, cut.channels), BF16)] * 2
    return call(functools.partial(inside_kernel, cut, last), "inside", (x, middle, *weights), [out], scratch)[0]


def half_weights(weights, side, half):
    rows = slice(half, 2 * half) if side else slice(0, half)
    order = [0, 1, 3, 4, 6, 7, 2, 5, 8]
    picked = [weights[tap, rows] for tap in order]
    return jnp.concatenate(picked + [jnp.zeros_like(picked[0])], 0)


def inside_half_kernel(cut, side, x, *refs):
    if side:
        middle, added, single, double, out, hi, lo = refs
    else:
        single, double, out, hi, lo = refs
    D, S, half = cut.D, cut.S, cut.half
    count, L, channels = out.shape
    gap = jnp.zeros((D, channels), F32)
    left = lax.broadcasted_iota(jnp.int32, (L, channels), 1) < half

    def pair(one, two):
        return jnp.where(left, one[side], two[1 - side])

    none = (jnp.zeros((L, channels), F32),) * 2

    def versions(slot):
        if not 1 <= slot <= S:
            return none, none, none
        row = x[slot - 1]
        both = (row, pltpu.roll(row, half, 1))
        sooner = tuple(jnp.concatenate([gap, v[:-D]], 0) for v in both)
        later = tuple(jnp.concatenate([v[D:], gap], 0) for v in both)
        return sooner, both, later

    following = versions(0)
    for slot in range(cut.slots):
        now, following = following, versions(slot + 1)
        for i, value in enumerate((pair(now[0], now[1]), pair(now[2], following[2]))):
            hi[i, slot], lo[i, slot] = split(value)
    first, _ = cut.range_of(False)

    def window(ref):
        columns = [(0, 0), (0, 1), (0, 2), (1, 0), (1, 2)]
        return jnp.concatenate(
            [jnp.concatenate([ref[i, first + j + a] for j in range(count)], 0) for i, a in columns], 1
        )

    y = multiply(window(hi), window(lo), *(half_weights(w, side, half) for w in (single, double)))
    y = shifted(y, D).reshape(count, L, channels)
    if not side:
        out[...] = y
        return
    out[...] = y + added[...]
    _, c, core = place()
    row = middle[...]
    parts = [split(v) for v in (jnp.concatenate([gap, row[:-D]], 0), row, jnp.concatenate([row[D:], gap], 0))]
    taps = pl.ds(jnp.where(core == 0, 6, 0), 3)
    one, two = (w[taps].reshape(3 * channels, -1) for w in (single, double))
    y = shifted(multiply(*(jnp.concatenate([p[i] for p in parts], 1) for i in range(2)), one, two), D)
    target = jnp.where(core == 0, count - 1, 0)
    out[target] += jnp.where(c == cut.C - 1, y, 0.0)


def inside_half(side, x, weights, cut, *more):
    count = cut.range_of(False)[1]
    L = cut.V * cut.D
    out = jax.ShapeDtypeStruct((count, L, cut.channels), F32)
    scratch = [pltpu.VMEM((2, cut.slots, L, cut.channels), BF16)] * 2
    body = functools.partial(inside_half_kernel, cut, side)
    cost = None if side else LITTLE
    return call(body, "inside_mirrored" if side else "inside_physical", (x, *more, *weights), [out], scratch, cost=cost)[0]


def add_planes(cut, last, target, offset, count, got_a, got_b, single, double, planes):
    D, V, pitch = cut.D, cut.V, cut.pitch
    z, Z = lax.axis_index("kz"), lax.axis_size("kz")
    odd = lax.rem(z, 2) == 1
    ends = jnp.logical_or(z == 0, z == Z - 1)
    first, _ = cut.range_of(last)
    height = -(-count * pitch // 16) * 16
    width = cut.H if last else V
    N, K = cut.channels, 9 * cut.channels
    got_a, got_b = got_a[...], jnp.where(ends, 0.0, got_b[...])
    for e, k, plane in ((0, 0, jnp.where(odd, got_a, got_b)), (2, D - 1, jnp.where(odd, got_b, got_a))):
        planes[...] = jnp.zeros_like(planes)
        for slot in range(cut.slots):
            column = plane[slot * V : (slot + 1) * V]
            for b in range(3):
                place = 8 + slot * pitch + 1 - b
                planes[b, place : place + V] = column
        parts = [
            split(planes[b, pl.ds(pl.multiple_of(8 + (first + a) * pitch, 8), height)])
            for a in range(3)
            for b in range(3)
        ]
        hi, lo = (jnp.concatenate([part[i] for part in parts], 1) for i in range(2))
        one = single[:, :, e * N : (e + 1) * N].reshape(K, N)
        two = double[:, :, 2 * e * N : (2 * e + 2) * N].reshape(K, 2 * N)
        (y,) = multiply(hi, lo, one, two)
        for i in range(count):
            target[offset + i, pl.ds(k, width, stride=D)] += y[i * pitch : i * pitch + width]


def planes_scratch(cut):
    return pltpu.VMEM((3, 8 + cut.slots * cut.pitch + 16, cut.channels), F32)


def middle_kernel(cut, x, marks, main, got_a, got_b, single, double, out, middle, planes):
    first, count = cut.range_of(False)
    out[...] = jnp.zeros_like(out)
    for i in range(count):
        out[first + i] = main[i]
    add_planes(cut, False, out, first, count, got_a, got_b, single, double, planes)
    out[...] = jnp.where(marks[...] > 0.5, x[...], out[...])
    middle[...] = middle_row(cut, out)


def last_kernel(cut, main, got_a, got_b, single, double, *rest):
    C, D, H, G, half = cut.C, cut.D, cut.H, cut.G, cut.half
    outs, (y, stage, planes) = rest[: 2 * C], rest[2 * C :]
    y[...] = main[...]
    add_planes(cut, True, y, 0, G, got_a, got_b, single, double, planes)
    flip = reversal(G * H)
    for k in range(D):
        rows = y[:, pl.ds(k, H, stride=D)].reshape(G * H, 2 * half).T
        stage[pl.ds(k, half, stride=D)] = rows[:half]
        hi, lo = split(rows[half:])
        stage[pl.ds(half * D + D - 1 - k, half, stride=D)] = dot(hi, flip) + dot(lo, flip)
    for d in range(C):
        for side in range(2):
            for ri in range(2):
                start = ((side * 2 + ri) * C + lax.bitwise_xor(lax.axis_index("coil"), d)) * cut.part
                start = pl.multiple_of(start, cut.part)
                outs[2 * d + side][ri * cut.part : (ri + 1) * cut.part] = stage[pl.ds(start, cut.part)]


def unpack_kernel(cut, d, measured, mask, own, mirrored, *refs):
    out, rows, sems = refs[-3:]
    ch, D, G, H = cut.ch, cut.D, cut.G, cut.H
    start = cut.piece(d) * G
    own, mirrored = (msg[...].reshape(ch, D, G * H) for msg in (own, mirrored))
    copies = []
    for j in range(G):
        sampled = (mask[start + j] == 1)[None]
        value = jnp.concatenate([msg[:, :, j * H : (j + 1) * H] for msg in (own, mirrored)], -1)
        rows[:, j] = jnp.where(sampled, measured[:, start + j], value)
        if j % 2:
            some = pl.ds(j - 1, 2)
            copy = pltpu.make_async_copy(rows.at[:, some], out.at[:, pl.ds(start + j - 1, 2)], sems.at[j // 2])
            copy.start()
            copies.append(copy)
    for copy in copies:
        copy.wait()


def unpack(d, measured, mask, msgs, cut, into=None):
    args = (measured, mask, *msgs) + (() if into is None else (into,))
    (out,) = call(
        functools.partial(unpack_kernel, cut, d),
        "unpack",
        args,
        [jax.ShapeDtypeStruct(measured.shape, F32)],
        [pltpu.VMEM((cut.ch, cut.G, cut.D, cut.W), F32), pltpu.SemaphoreType.DMA((cut.G // 2,))],
        far=() if into is None else (len(args) - 1,),
        out=ANY,
        input_output_aliases={} if into is None else {len(args) - 1: 0},
    )
    return out


def on_device(measured, mask, kernel):
    Z, C, X = (lax.axis_size(axis) for axis in AXES)
    every = [(z, c, x) for z in range(Z) for c in range(C) for x in range(X)]

    def index(z, c, x):
        return (z * C + c) * X + x

    def send(array, target):
        return lax.ppermute(array, AXES, [(index(*p), index(*target(*p))) for p in every])

    def exchange(msgs):
        got = list(msgs)
        for d in range(C):
            got[2 * d + 1] = send(msgs[2 * d + 1], lambda z, c, x: (Z - 1 - z, c ^ d, X - 1 - x))
        for d in range(1, C):
            got[2 * d] = send(msgs[2 * d], lambda z, c, x: (z, c ^ d, x))
        return got

    def plane_a(z, c, x):
        return (z ^ 1, c, x)

    def plane_b(z, c, x):
        other = z + 1 if z % 2 else z - 1
        return (other, c, x) if 0 <= other < Z else (z, c, X - 1 - x)

    def core(z, c, x):
        return (z, c, X - 1 - x)

    parts, coils, rows, D, W = measured.shape
    cut = Cut(rows, D, W, C, 2 * parts * coils * C)
    flat = measured.reshape(parts * coils, rows, D, W)
    kernel = kernel.reshape(-1, *kernel.shape[2:])
    msgs = []
    for d in reversed(range(C)):
        msgs = [*pack(d, flat, mask, cut), *msgs]
        kernel, mask, *msgs = lax.optimization_barrier((kernel, mask, *msgs)) if d else (kernel, mask, *msgs)
    msgs = exchange(msgs)
    folded = []
    for d in range(1, C):
        half = send(fold(kernel), lambda z, c, x: (z, c ^ d, x))
        folded += [half, send(half, core)]
    weights = build_weights(kernel, folded, cut)
    state, marks, row, added = points(cut, weights, msgs)
    for step in range(ITERS):
        last = step == ITERS - 1
        row = send(row, core)
        face_a, face_b = faces(state, row, cut)
        got_a, got_b = send(face_a, plane_a), send(face_b, plane_b)
        main = inside(state, row, weights, cut, last) if step else inside_half(1, state, weights, cut, row, added)
        if not last:
            state, row = call(
                functools.partial(middle_kernel, cut),
                "middle",
                (state, marks, main, got_a, got_b, *weights),
                [jax.ShapeDtypeStruct(state.shape, F32), jax.ShapeDtypeStruct(row.shape, F32)],
                [planes_scratch(cut)],
            )
    message = jax.ShapeDtypeStruct((cut.ch * D, cut.G * cut.H), F32)
    msgs = call(
        functools.partial(last_kernel, cut),
        "last",
        (main, got_a, got_b, *weights),
        [message] * (2 * C),
        [pltpu.VMEM(main.shape, F32), pltpu.VMEM((cut.channels * D, cut.G * cut.H), F32), planes_scratch(cut)],
    )
    msgs = exchange(msgs)
    out = None
    for d in range(C):
        out = unpack(d, flat, mask, msgs[2 * d : 2 * d + 2], cut, out)
    return out.reshape(measured.shape)


def solution(mesh):
    placed = (
        P(None, ("grp", "coil"), "kx", "kz", None),
        P(("grp", "kx"), "kz", None),
        P(None, None, "coil", None),
    )
    return jax.shard_map(
        on_device,
        mesh=mesh,
        in_specs=placed,
        out_specs=P(None, ("grp", "coil"), "kx", "kz", None),
        check_vma=False,
    )
```

```python
import functools

import jax
import jax.numpy as jnp
from jax import lax
from jax.experimental import pallas as pl
from jax.experimental.pallas import tpu as pltpu
from jax.sharding import PartitionSpec as P

PACK = 56 << 20
LITTLE = pl.CostEstimate(flops=1000, bytes_accessed=1000, transcendentals=0)
AXES = ("kz", "coil", "kx")
F32 = jnp.float32
BF16 = jnp.bfloat16
ANY = pl.BlockSpec(memory_space=pl.ANY)
HBM = pl.BlockSpec(memory_space=pltpu.HBM)
VMEM = pl.BlockSpec(memory_space=pltpu.VMEM)


def call(body, name, args, shapes, scratch=(), far=(), space=ANY, out=VMEM, limit=32 << 20, cost=None, **options):
    return pl.pallas_call(
        body,
        out_shape=shapes,
        in_specs=[space if i in far else VMEM for i in range(len(args))],
        out_specs=[out] * len(shapes),
        scratch_shapes=list(scratch),
        compiler_params=pltpu.CompilerParams(vmem_limit_bytes=limit),
        cost_estimate=cost,
        name=name,
        **options,
    )(*args)


def split(x):
    hi = x.astype(BF16)
    return hi, (x - hi.astype(F32)).astype(BF16)


def reversal(n):
    row = lax.broadcasted_iota(jnp.int32, (n, n), 0)
    column = lax.broadcasted_iota(jnp.int32, (n, n), 1)
    return jnp.where(row + column == n - 1, 1.0, 0.0).astype(BF16)


def dot(a, b):
    return jnp.dot(a, b, preferred_element_type=F32)


class Cut:
    def __init__(self, rows, D, W, C, channels):
        self.rows, self.D, self.W, self.C = rows, D, W, C
        self.channels = channels
        self.half = channels // 2
        self.ch = self.half // C
        self.G = rows // C
        self.S = min(rows, self.G + (2 if C == 2 else 4))
        self.H = W // 2
        self.V = self.H + 2
        self.base = 128 // self.H
        self.spare = (self.S - self.base) * self.H
        self.part = self.ch // 2 * D
        self.used = self.spare + 2 * self.S
        self.group = self.ch * D // 16
        self.folds = -(-16 * self.used // 128)
        self.length = 2 * self.part + self.folds * self.group
        self.pitch = -(-(self.V + 1) // 8) * 8

    def piece(self, d=0):
        c, x = lax.bitwise_xor(lax.axis_index("coil"), d), lax.axis_index("kx")
        return jnp.where(x == 0, c, self.C - 1 - c)

    def start(self, d=0):
        return jnp.clip(self.G * self.piece(d) - 2, 0, self.rows - self.S)

    def own(self):
        return self.G * self.piece() - self.start()


def place():
    return tuple(lax.axis_index(axis) for axis in AXES)


def arrangement(cut):
    S, H, W = cut.S, cut.H, cut.W
    shift = H.bit_length() - 1
    j = lax.broadcasted_iota(jnp.int32, (1, 384), 1)
    own = j - jnp.where(j >= 320, 320, jnp.where(j >= 256, 256, jnp.where(j >= 128, 128, 0)))
    spare = j >= 256
    row = lax.shift_right_logical(own, shift)
    main = row * W + lax.bitwise_and(own, H - 1)
    rest = own - cut.spare
    edge = lax.shift_right_logical(rest, 1) * W + H + lax.bitwise_and(rest, 1)
    source = jnp.where(spare, jnp.where(own < cut.spare, main + cut.base * W, edge), main)
    mirrored = jnp.logical_or(jnp.logical_and(j >= 128, j < 256), j >= 320)
    source = jnp.where(mirrored, S * W - 1 - source, source)
    source = jnp.where(jnp.logical_and(spare, rest >= 2 * S), -1, source)
    lane = lax.broadcasted_iota(jnp.int32, (S * W, 384), 0)
    return jnp.where(lane == source, 1.0, 0.0).astype(BF16)


def pack_kernel(cut, d, measured, mask, *refs):
    S, ch, D, W, part = cut.S, cut.ch, cut.D, cut.W, cut.part
    outs, (rows, marks, sems) = refs[:2], refs[2:]
    start = cut.start(d)
    copies = [pltpu.make_async_copy(mask.at[pl.ds(start, S)], marks, sems.at[0])]
    copies.append(pltpu.make_async_copy(measured.at[:, pl.ds(start, S)], rows, sems.at[1]))
    for copy in copies:
        copy.start()
    order = arrangement(cut)
    for copy in copies:
        copy.wait()
    sampled = [marks[j] == 1 for j in range(S)]
    kept = [jnp.where(sampled[j][None], rows[:, j], 0.0) for j in range(S)]
    kept = jnp.concatenate(kept, -1).reshape(ch * D, S * W)
    if d < 2:
        kept = jnp.concatenate([kept, jnp.concatenate([jnp.where(s, 1.0, 0.0) for s in sampled], -1)], 0)
    hi, lo = split(kept)
    y = dot(hi, order) + dot(lo, order)
    for side in (1, 0):
        out = outs[side]
        out[: 2 * part] = y[: 2 * part, 128 * side : 128 * side + 128]
        spare = y[:, 256 + 64 * side : 320 + 64 * side]
        group = cut.group
        folded = [spare[i * group : (i + 1) * group, : cut.used] for i in range(16)]
        if cut.folds * 128 > 16 * cut.used:
            folded.append(jnp.zeros((group, cut.folds * 128 - 16 * cut.used), F32))
        folded = jnp.concatenate(folded, 1)
        for i in range(cut.folds):
            place = 2 * part + i * group
            out[place : place + group] = folded[:, i * 128 : (i + 1) * 128]
        if d == side:
            out[cut.length : cut.length + D] = y[2 * part :, 128 * side : 128 * side + 128]
            out[cut.length + D :] = jnp.concatenate([spare[2 * part :], jnp.zeros((D, 64), F32)], 1)


def pack(d, measured, mask, cut):
    shapes = [jax.ShapeDtypeStruct((cut.length + (2 * cut.D if d == side else 0), 128), F32) for side in range(2)]
    scratch = [
        pltpu.VMEM((cut.ch, cut.S, cut.D, cut.W), F32),
        pltpu.VMEM((cut.S, cut.D, cut.W), jnp.int32),
        pltpu.SemaphoreType.DMA((2,)),
    ]
    body = functools.partial(pack_kernel, cut, d)
    return call(body, "pack", (measured, mask), shapes, scratch, far=(0, 1), space=HBM, limit=PACK)


def fold_kernel(kernel, out):
    count = out.shape[0]
    half = kernel.shape[1] // 2
    some = kernel[pl.ds(lax.axis_index("kx") * count, count)]
    out[...] = jnp.concatenate([some[:, :half], some[:, half:]], -1)


def fold(kernel):
    count, coils, inputs = kernel.shape
    shape = jax.ShapeDtypeStruct((count // 2, coils // 2, 2 * inputs), F32)
    return call(fold_kernel, "fold", (kernel,), [shape])[0]


def weights_kernel(cut, own, *refs):
    folded, (single, double, kernel) = refs[:-3], refs[-3:]
    count, coils, inputs = kernel.shape
    local = coils // cut.C
    c, x = lax.axis_index("coil"), lax.axis_index("kx")
    kernel[:, pl.ds(pl.multiple_of(c * local, local), local)] = own[...]
    for i, half in enumerate(folded):
        d, other = i // 2 + 1, i % 2
        place = pl.multiple_of(lax.bitwise_xor(c, d) * local, local)
        taps = pl.ds(lax.bitwise_xor(x, other) * (count // 2), count // 2)
        kernel[taps, pl.ds(place, local // 2)] = half[..., :inputs]
        kernel[taps, pl.ds(place + local // 2, local // 2)] = half[..., inputs:]

    def parts(tap):
        re, im = kernel[2 * tap], kernel[2 * tap + 1]
        return re[:, :coils], im[:, :coils], re[:, coils:], im[:, coils:]

    N = 4 * coils
    taps = count // 2
    for t in range(taps):
        pr, pi, vr, vi = parts(t)
        qr, qi, ur, ui = parts(taps - 1 - t)
        block = jnp.concatenate(
            [
                jnp.concatenate([pr, -pi, vr, vi], 1),
                jnp.concatenate([pi, pr, vi, -vr], 1),
                jnp.concatenate([ur, ui, qr, -qi], 1),
                jnp.concatenate([ui, -ur, qi, qr], 1),
            ],
            0,
        ).T
        hi, lo = split(block)
        e, tap = t % 3, t // 3
        single[tap, :, e * N : (e + 1) * N] = hi
        double[tap, :, 2 * e * N : (2 * e + 1) * N] = hi
        double[tap, :, (2 * e + 1) * N : (2 * e + 2) * N] = lo


def build_weights(kernel, folded, cut):
    count, coils, inputs = kernel.shape
    N = cut.channels
    shapes = [jax.ShapeDtypeStruct((9, N, 3 * N), BF16), jax.ShapeDtypeStruct((9, N, 6 * N), BF16)]
    scratch = [pltpu.VMEM((count, coils * cut.C, inputs), F32)]
    return call(functools.partial(weights_kernel, cut), "weights", (kernel, *folded), shapes, scratch, cost=LITTLE)


def spread(cut, target, k, first, rest):
    D, H, S = cut.D, cut.H, cut.S
    if k == 0:
        for r in (0, 1, S + 2, S + 3):
            target[r] = jnp.zeros(target.shape[1:], F32)
    for r in range(cut.base):
        target[r + 2, pl.ds(k, H, stride=D)] = first[r * H : (r + 1) * H]
    for r in range(cut.base, S):
        target[r + 2, pl.ds(k, H, stride=D)] = rest[(r - cut.base) * H : (r - cut.base + 1) * H]
    for r in range(S):
        place = cut.spare + 2 * r
        target[r + 2, pl.ds(H * D + k, 2, stride=D)] = rest[place : place + 2]


def assemble(cut, side, msgs, x, main, spare):
    D, half, part = cut.D, cut.half, cut.part
    for d, msg in enumerate(msgs):
        other = lax.bitwise_xor(lax.axis_index("coil"), d)
        folded = msg[2 * part : cut.length].reshape(cut.folds, cut.group, 128)
        folded = jnp.concatenate([folded[i] for i in range(cut.folds)], 1)
        for ri in range(2):
            start = pl.multiple_of((ri * cut.C + other) * part, part)
            main[pl.ds(start, part)] = msg[ri * part : (ri + 1) * part]
        for i in range(16):
            start = pl.multiple_of((i // 8 * cut.C + other) * part + i % 8 * cut.group, cut.group)
            spare[pl.ds(start, cut.group), : cut.used] = folded[:, i * cut.used : (i + 1) * cut.used]
    gap = jnp.zeros((half, 128), F32)
    for k in range(D):
        some = pl.ds(D - 1 - k if side else k, half, stride=D)
        blocks = [jnp.concatenate([gap, v] if side else [v, gap], 0).T for v in (main[some], spare[some])]
        spread(cut, x, k, *blocks)


def physical_kernel(cut, ready, *refs):
    msgs, (x, main, spare) = refs[: cut.C], refs[cut.C :]
    assemble(cut, 0, msgs, x, main, spare)


def mirrored_kernel(cut, physical, marks, *refs):
    msgs, (x, rows, main, spare) = refs[: cut.C], refs[-4:]
    assemble(cut, 1, msgs, x, main, spare)
    x[...] = x[...] + physical[...]
    lower, S = lax.axis_index("kx") == 0, cut.S
    rows[0] = jnp.where(lower, x[S + 1], x[2])
    rows[1] = jnp.where(lower, x[S], x[3])
    rows[2] = jnp.where(lower, marks[S + 1], marks[2])


def marks_kernel(cut, ready, own, other, marks):
    D, half = cut.D, cut.half
    lane = lax.broadcasted_iota(jnp.int32, (128, cut.channels), 1)
    flags = [msg[cut.length : cut.length + 2 * D] for msg in (own, other)]
    flags = jnp.concatenate(flags + [jnp.zeros((128 - 4 * D, 128), F32)], 0).T
    for k in range(D):
        j = D - 1 - k
        first = jnp.where(lane < half, flags[:, k : k + 1], flags[:, 2 * D + j : 2 * D + j + 1])
        rest = jnp.where(lane < half, flags[:, D + k : D + k + 1], flags[:, 3 * D + j : 3 * D + j + 1])
        spread(cut, marks, k, first, rest)


def points(cut, weights, msgs):
    row = (cut.V * cut.D, cut.channels)
    window = jax.ShapeDtypeStruct((cut.S + 4, *row), F32)
    stages = [pltpu.VMEM((cut.half * cut.D, 128), F32)] * 2
    args = (weights[0], *msgs[0::2])
    (x,) = call(functools.partial(physical_kernel, cut), "physical", args, [window], stages, far=(0,), cost=LITTLE)
    added = inside_half(0, x, weights, cut)
    flags = (added, msgs[0], msgs[3])
    (marks,) = call(functools.partial(marks_kernel, cut), "marks", flags, [window], far=(0,), cost=LITTLE)
    args = (x, marks, *msgs[1::2])
    x, rows = call(
        functools.partial(mirrored_kernel, cut),
        "mirrored",
        args,
        [window, jax.ShapeDtypeStruct((3, *row), F32)],
        stages,
    )
    return x, marks, rows, added


def edges(cut):
    _, c, x = place()
    inner = c == cut.C - 1
    return jnp.logical_and(inner, x == 1), jnp.logical_and(inner, x == 0)


def put_faces(cut, slot, row, face_a, face_b):
    D, V = cut.D, cut.V
    odd = lax.rem(lax.axis_index("kz"), 2) == 1
    first, final = row(pl.ds(0, V, stride=D)), row(pl.ds(D - 1, V, stride=D))
    face_a[slot * V : (slot + 1) * V] = jnp.where(odd, first, final)
    face_b[slot * V : (slot + 1) * V] = jnp.where(odd, final, first)


def faces_kernel(cut, x, rows, face_a, face_b):
    own, G = cut.own(), cut.G
    before, after = edges(cut)
    other = {0: (before, 1), 1: (before, 0), G + 2: (after, 0), G + 3: (after, 1)}
    for slot in range(G + 4):

        def row(some):
            value = x[own + slot, some]
            if slot in other:
                there, which = other[slot]
                value = jnp.where(there, rows[which, some], value)
            return value

        put_faces(cut, slot, row, face_a, face_b)


def faces(x, rows, cut):
    face = jax.ShapeDtypeStruct(((cut.G + 4) * cut.V, cut.channels), F32)
    return call(functools.partial(faces_kernel, cut), "faces", (x, rows), [face, face])


def multiply(hi, lo, single, double):
    N = single.shape[-1]
    groups = double.shape[-1] // (2 * 128)
    y, z = dot(hi, double), dot(lo, single)
    N = N // groups
    return [
        y[:, 2 * e * N : (2 * e + 1) * N] + y[:, (2 * e + 1) * N : (2 * e + 2) * N] + z[:, e * N : (e + 1) * N]
        for e in range(groups)
    ]


def shifted(y, D):
    M = y[0].shape[0]
    rows = lax.broadcasted_iota(jnp.int32, y[0].shape, 0) % D
    later = jnp.where(rows == 0, 0.0, pltpu.roll(y[0], 1, 0))
    sooner = jnp.where(rows == D - 1, 0.0, pltpu.roll(y[2], M - 1, 0))
    return y[1] + later + sooner


def inside_kernel(cut, x, single, double, out, hi, lo):
    D = cut.D
    count, L, channels = out.shape
    gap = jnp.zeros((D, channels), F32)
    for slot in range(count + 2):
        row = x[slot]
        high = row.astype(BF16).astype(F32)
        for ref, value in ((hi, high), (lo, row - high)):
            ref[0, slot] = jnp.concatenate([gap, value[:-D]], 0).astype(BF16)
            ref[1, slot] = value.astype(BF16)
            ref[2, slot] = jnp.concatenate([value[D:], gap], 0).astype(BF16)

    def window(ref):
        return jnp.concatenate(
            [jnp.concatenate([ref[b, i + a, :L] for i in range(count)], 0) for a in range(3) for b in range(3)], 1
        )

    K = 9 * channels
    y = multiply(window(hi), window(lo), single[...].reshape(K, -1), double[...].reshape(K, -1))
    out[...] = shifted(y, D).reshape(count, L, channels)


def inside(x, weights, cut):
    out = jax.ShapeDtypeStruct((cut.G, cut.H * cut.D, cut.channels), F32)
    scratch = [pltpu.VMEM((3, cut.G + 2, cut.V * cut.D, cut.channels), BF16)] * 2
    return call(functools.partial(inside_kernel, cut), "inside", (x, *weights), [out], scratch)[0]


def half_weights(weights, side, half):
    rows = slice(half, 2 * half) if side else slice(0, half)
    order = [0, 1, 3, 4, 6, 7, 2, 5, 8]
    picked = [weights[tap, rows] for tap in order]
    return jnp.concatenate(picked + [jnp.zeros_like(picked[0])], 0)


def inside_half_kernel(cut, side, x, *refs):
    if side:
        rows, added, single, double, out, hi, lo = refs
    else:
        single, double, out, hi, lo = refs
    D, half, own = cut.D, cut.half, cut.own()
    count, L, channels = out.shape
    gap = jnp.zeros((D, channels), F32)
    left = lax.broadcasted_iota(jnp.int32, (L, channels), 1) < half

    def pair(one, two):
        return jnp.where(left, one[side], two[1 - side])

    none = (jnp.zeros((L, channels), F32),) * 2

    def versions(slot):
        if slot == count + 2:
            return none, none, none
        row = x[own + slot]
        both = (row, pltpu.roll(row, half, 1))
        sooner = tuple(jnp.concatenate([gap, v[:-D]], 0) for v in both)
        later = tuple(jnp.concatenate([v[D:], gap], 0) for v in both)
        return sooner, both, later

    following = versions(0)
    for slot in range(count + 2):
        now, following = following, versions(slot + 1)
        for i, value in enumerate((pair(now[0], now[1]), pair(now[2], following[2]))):
            hi[i, slot], lo[i, slot] = split(value)

    def window(ref):
        columns = [(0, 0), (0, 1), (0, 2), (1, 0), (1, 2)]
        return jnp.concatenate(
            [jnp.concatenate([ref[i, j + a] for j in range(count)], 0) for i, a in columns], 1
        )

    y = multiply(window(hi), window(lo), *(half_weights(w, side, half) for w in (single, double)))
    y = shifted(y, D).reshape(count, L, channels)
    if not side:
        out[...] = y
        return
    out[...] = y + added[...]
    before, after = edges(cut)
    lower = lax.axis_index("kx") == 0
    pieces = []
    for row in (rows[0], rows[1]):
        parts = [split(v) for v in (jnp.concatenate([gap, row[:-D]], 0), row, jnp.concatenate([row[D:], gap], 0))]
        pieces.append([jnp.concatenate([p[i] for p in parts], 1) for i in range(2)])
    near, second = pieces
    wide = [
        jnp.concatenate([jnp.concatenate([n, f], 1), jnp.concatenate([jnp.zeros_like(n), n], 1)], 0)
        for n, f in zip(near, second)
    ]
    outer = pl.ds(jnp.where(lower, 6, 0), 3)
    taps = [jnp.concatenate([w[3:6], w[outer]], 0).reshape(6 * channels, -1) for w in (single, double)]
    y = shifted(multiply(*wide, *taps), D)
    there = jnp.logical_or(before, after)
    for i in range(2):
        target = jnp.where(lower, count - 1 - i, i)
        out[target] += jnp.where(there, y[i * L : (i + 1) * L], 0.0)


def inside_half(side, x, weights, cut, *more):
    count, L = cut.G + 2, cut.V * cut.D
    out = jax.ShapeDtypeStruct((count, L, cut.channels), F32)
    scratch = [pltpu.VMEM((2, count + 2, L, cut.channels), BF16)] * 2
    body = functools.partial(inside_half_kernel, cut, side)
    cost = None if side else LITTLE
    return call(body, "inside_mirrored" if side else "inside_physical", (x, *more, *weights), [out], scratch, cost=cost)[0]


def add_planes(cut, width, target, got_a, got_b, single, double, planes):
    D, V, pitch = cut.D, cut.V, cut.pitch
    z, Z = lax.axis_index("kz"), lax.axis_size("kz")
    odd = lax.rem(z, 2) == 1
    ends = jnp.logical_or(z == 0, z == Z - 1)
    count = target.shape[0]
    height = -(-count * pitch // 16) * 16
    N, K = cut.channels, 9 * cut.channels
    got_a, got_b = got_a[...], jnp.where(ends, 0.0, got_b[...])
    for e, k, plane in ((0, 0, jnp.where(odd, got_a, got_b)), (2, D - 1, jnp.where(odd, got_b, got_a))):
        planes[...] = jnp.zeros_like(planes)
        for slot in range(count + 2):
            column = plane[slot * V : (slot + 1) * V]
            for b in range(3):
                place = 8 + slot * pitch + 1 - b
                planes[b, place : place + V] = column
        parts = [
            split(planes[b, 8 + a * pitch : 8 + a * pitch + height])
            for a in range(3)
            for b in range(3)
        ]
        hi, lo = (jnp.concatenate([part[i] for part in parts], 1) for i in range(2))
        one = single[:, :, e * N : (e + 1) * N].reshape(K, N)
        two = double[:, :, 2 * e * N : (2 * e + 2) * N].reshape(K, 2 * N)
        (y,) = multiply(hi, lo, one, two)
        for i in range(count):
            target[i, pl.ds(k, width, stride=D)] += y[i * pitch : i * pitch + width]


def planes_scratch(cut, count):
    return pltpu.VMEM((3, 8 + (count + 2) * cut.pitch + 16, cut.channels), F32)


def middle_kernel(cut, x, marks, rows, main, got_a, got_b, single, double, out, face_a, face_b, planes):
    G, own = cut.G, cut.own()
    before, after = edges(cut)
    core, piece = lax.axis_index("kx"), cut.piece()
    out[...] = main[...]
    add_planes(cut, cut.V, out, got_a, got_b, single, double, planes)
    first = jnp.logical_and(core == 0, piece == 0)
    final = jnp.logical_and(core == 1, piece == cut.C - 1)
    for i in range(G + 2):
        kept, mark = x[own + 1 + i], marks[own + 1 + i]
        if i in (0, G + 1):
            there, outside = (before, first) if i == 0 else (after, final)
            kept, mark = jnp.where(there, rows[0], kept), jnp.where(there, rows[2], mark)
            value = jnp.where(outside, 0.0, jnp.where(mark > 0.5, kept, out[i]))
        else:
            value = jnp.where(mark > 0.5, kept, out[i])
        out[i] = value
        put_faces(cut, i, lambda some: out[i, some], face_a, face_b)


def last_kernel(cut, main, got_a, got_b, single, double, *rest):
    C, D, H, G, half = cut.C, cut.D, cut.H, cut.G, cut.half
    outs, (y, stage, planes) = rest[: 2 * C], rest[2 * C :]
    y[...] = main[...]
    add_planes(cut, H, y, got_a, got_b, single, double, planes)
    flip = reversal(G * H)
    for k in range(D):
        rows = y[:, pl.ds(k, H, stride=D)].reshape(G * H, 2 * half).T
        stage[pl.ds(k, half, stride=D)] = rows[:half]
        hi, lo = split(rows[half:])
        stage[pl.ds(half * D + D - 1 - k, half, stride=D)] = dot(hi, flip) + dot(lo, flip)
    for d in range(C):
        for side in range(2):
            for ri in range(2):
                start = ((side * 2 + ri) * C + lax.bitwise_xor(lax.axis_index("coil"), d)) * cut.part
                start = pl.multiple_of(start, cut.part)
                outs[2 * d + side][ri * cut.part : (ri + 1) * cut.part] = stage[pl.ds(start, cut.part)]


def unpack_kernel(cut, d, measured, mask, own, mirrored, *refs):
    out, rows, sems = refs[-3:]
    ch, D, G, H = cut.ch, cut.D, cut.G, cut.H
    start = cut.piece(d) * G
    own, mirrored = (msg[...].reshape(ch, D, G * H) for msg in (own, mirrored))
    copies = []
    for j in range(G):
        sampled = (mask[start + j] == 1)[None]
        value = jnp.concatenate([msg[:, :, j * H : (j + 1) * H] for msg in (own, mirrored)], -1)
        rows[:, j] = jnp.where(sampled, measured[:, start + j], value)
        if j % 2:
            some = pl.ds(j - 1, 2)
            copy = pltpu.make_async_copy(rows.at[:, some], out.at[:, pl.ds(start + j - 1, 2)], sems.at[j // 2])
            copy.start()
            copies.append(copy)
    for copy in copies:
        copy.wait()


def unpack(d, measured, mask, msgs, cut, into=None):
    args = (measured, mask, *msgs) + (() if into is None else (into,))
    (out,) = call(
        functools.partial(unpack_kernel, cut, d),
        "unpack",
        args,
        [jax.ShapeDtypeStruct(measured.shape, F32)],
        [pltpu.VMEM((cut.ch, cut.G, cut.D, cut.W), F32), pltpu.SemaphoreType.DMA((cut.G // 2,))],
        far=() if into is None else (len(args) - 1,),
        out=ANY,
        input_output_aliases={} if into is None else {len(args) - 1: 0},
    )
    return out


def on_device(measured, mask, kernel):
    Z, C, X = (lax.axis_size(axis) for axis in AXES)
    every = [(z, c, x) for z in range(Z) for c in range(C) for x in range(X)]

    def index(z, c, x):
        return (z * C + c) * X + x

    def send(array, target):
        return lax.ppermute(array, AXES, [(index(*p), index(*target(*p))) for p in every])

    def exchange(msgs):
        got = list(msgs)
        for d in range(C):
            got[2 * d + 1] = send(msgs[2 * d + 1], lambda z, c, x: (Z - 1 - z, c ^ d, X - 1 - x))
        for d in range(1, C):
            got[2 * d] = send(msgs[2 * d], lambda z, c, x: (z, c ^ d, x))
        return got

    def plane_a(z, c, x):
        return (z ^ 1, c, x)

    def plane_b(z, c, x):
        other = z + 1 if z % 2 else z - 1
        return (other, c, x) if 0 <= other < Z else (z, c, X - 1 - x)

    def core(z, c, x):
        return (z, c, X - 1 - x)

    parts, coils, rows, D, W = measured.shape
    cut = Cut(rows, D, W, C, 2 * parts * coils * C)
    flat = measured.reshape(parts * coils, rows, D, W)
    kernel = kernel.reshape(-1, *kernel.shape[2:])
    msgs = []
    for d in reversed(range(C)):
        msgs = [*pack(d, flat, mask, cut), *msgs]
        kernel, mask, *msgs = lax.optimization_barrier((kernel, mask, *msgs)) if d else (kernel, mask, *msgs)
    msgs = exchange(msgs)
    folded = []
    for d in range(1, C):
        half = send(fold(kernel), lambda z, c, x: (z, c ^ d, x))
        folded += [half, send(half, core)]
    weights = build_weights(kernel, folded, cut)
    state, marks, near, added = points(cut, weights, msgs)
    near = send(near, core)
    got = [send(face, to) for face, to in zip(faces(state, near, cut), (plane_a, plane_b))]
    main = inside_half(1, state, weights, cut, near, added)
    face = jax.ShapeDtypeStruct(((cut.G + 2) * cut.V, cut.channels), F32)
    state, *sides = call(
        functools.partial(middle_kernel, cut),
        "middle",
        (state, marks, near, main, *got, *weights),
        [jax.ShapeDtypeStruct(main.shape, F32), face, face],
        [planes_scratch(cut, cut.G + 2)],
    )
    got = [send(face, to) for face, to in zip(sides, (plane_a, plane_b))]
    main = inside(state, weights, cut)
    message = jax.ShapeDtypeStruct((cut.ch * D, cut.G * cut.H), F32)
    msgs = call(
        functools.partial(last_kernel, cut),
        "last",
        (main, *got, *weights),
        [message] * (2 * C),
        [pltpu.VMEM(main.shape, F32), pltpu.VMEM((cut.channels * D, cut.G * cut.H), F32), planes_scratch(cut, cut.G)],
    )
    msgs = exchange(msgs)
    out = None
    for d in range(C):
        out = unpack(d, flat, mask, msgs[2 * d : 2 * d + 2], cut, out)
    return out.reshape(measured.shape)


def solution(mesh):
    placed = (
        P(None, ("grp", "coil"), "kx", "kz", None),
        P(("grp", "kx"), "kz", None),
        P(None, None, "coil", None),
    )
    return jax.shard_map(
        on_device,
        mesh=mesh,
        in_specs=placed,
        out_specs=P(None, ("grp", "coil"), "kx", "kz", None),
        check_vma=False,
    )
```

```python
import functools

import jax
import jax.numpy as jnp
from jax import lax
from jax.experimental import pallas as pl
from jax.experimental.pallas import tpu as pltpu
from jax.sharding import PartitionSpec as P

PACK = 56 << 20
LITTLE = pl.CostEstimate(flops=1000, bytes_accessed=1000, transcendentals=0)
AXES = ("kz", "coil", "kx")
F32 = jnp.float32
BF16 = jnp.bfloat16
ANY = pl.BlockSpec(memory_space=pl.ANY)
HBM = pl.BlockSpec(memory_space=pltpu.HBM)
VMEM = pl.BlockSpec(memory_space=pltpu.VMEM)


def call(body, name, args, shapes, scratch=(), far=(), space=ANY, out=VMEM, limit=32 << 20, cost=None, **options):
    return pl.pallas_call(
        body,
        out_shape=shapes,
        in_specs=[space if i in far else VMEM for i in range(len(args))],
        out_specs=[out] * len(shapes),
        scratch_shapes=list(scratch),
        compiler_params=pltpu.CompilerParams(vmem_limit_bytes=limit),
        cost_estimate=cost,
        name=name,
        **options,
    )(*args)


def split(x):
    hi = x.astype(BF16)
    return hi, (x - hi.astype(F32)).astype(BF16)


def reversal(n):
    row = lax.broadcasted_iota(jnp.int32, (n, n), 0)
    column = lax.broadcasted_iota(jnp.int32, (n, n), 1)
    return jnp.where(row + column == n - 1, 1.0, 0.0).astype(BF16)


def dot(a, b):
    return jnp.dot(a, b, preferred_element_type=F32)


class Cut:
    def __init__(self, rows, D, W, C, channels):
        self.rows, self.D, self.W, self.C = rows, D, W, C
        self.channels = channels
        self.half = channels // 2
        self.ch = self.half // C
        self.G = rows // C
        self.S = min(rows, self.G + (2 if C == 2 else 4))
        self.H = W // 2
        self.V = self.H + 2
        self.base = 128 // self.H
        self.spare = (self.S - self.base) * self.H
        self.part = self.ch // 2 * D
        self.used = self.spare + 2 * self.S
        self.group = self.ch * D // 16
        self.folds = -(-16 * self.used // 128)
        self.length = 2 * self.part + self.folds * self.group
        self.pitch = -(-(self.V + 1) // 8) * 8

    def piece(self, d=0):
        c, x = lax.bitwise_xor(lax.axis_index("coil"), d), lax.axis_index("kx")
        return jnp.where(x == 0, c, self.C - 1 - c)

    def start(self, d=0):
        return jnp.clip(self.G * self.piece(d) - 2, 0, self.rows - self.S)

    def own(self):
        return self.G * self.piece() - self.start()


def place():
    return tuple(lax.axis_index(axis) for axis in AXES)


def arrangement(cut):
    S, H, W = cut.S, cut.H, cut.W
    shift = H.bit_length() - 1
    j = lax.broadcasted_iota(jnp.int32, (1, 384), 1)
    own = j - jnp.where(j >= 320, 320, jnp.where(j >= 256, 256, jnp.where(j >= 128, 128, 0)))
    spare = j >= 256
    row = lax.shift_right_logical(own, shift)
    main = row * W + lax.bitwise_and(own, H - 1)
    rest = own - cut.spare
    edge = lax.shift_right_logical(rest, 1) * W + H + lax.bitwise_and(rest, 1)
    source = jnp.where(spare, jnp.where(own < cut.spare, main + cut.base * W, edge), main)
    mirrored = jnp.logical_or(jnp.logical_and(j >= 128, j < 256), j >= 320)
    source = jnp.where(mirrored, S * W - 1 - source, source)
    source = jnp.where(jnp.logical_and(spare, rest >= 2 * S), -1, source)
    lane = lax.broadcasted_iota(jnp.int32, (S * W, 384), 0)
    return jnp.where(lane == source, 1.0, 0.0).astype(BF16)


def pack_kernel(cut, d, measured, mask, *refs):
    S, ch, D, W, part = cut.S, cut.ch, cut.D, cut.W, cut.part
    outs, (rows, marks, sems) = refs[:2], refs[2:]
    start = cut.start(d)
    copies = [pltpu.make_async_copy(mask.at[pl.ds(start, S)], marks, sems.at[0])]
    copies.append(pltpu.make_async_copy(measured.at[:, pl.ds(start, S)], rows, sems.at[1]))
    for copy in copies:
        copy.start()
    order = arrangement(cut)
    for copy in copies:
        copy.wait()
    sampled = [marks[j] == 1 for j in range(S)]
    kept = [jnp.where(sampled[j][None], rows[:, j], 0.0) for j in range(S)]
    kept = jnp.concatenate(kept, -1).reshape(ch * D, S * W)
    if d < 2:
        kept = jnp.concatenate([kept, jnp.concatenate([jnp.where(s, 1.0, 0.0) for s in sampled], -1)], 0)
    hi, lo = split(kept)
    y = dot(hi, order) + dot(lo, order)
    for side in (1, 0):
        out = outs[side]
        out[: 2 * part] = y[: 2 * part, 128 * side : 128 * side + 128]
        spare = y[:, 256 + 64 * side : 320 + 64 * side]
        group = cut.group
        folded = [spare[i * group : (i + 1) * group, : cut.used] for i in range(16)]
        if cut.folds * 128 > 16 * cut.used:
            folded.append(jnp.zeros((group, cut.folds * 128 - 16 * cut.used), F32))
        folded = jnp.concatenate(folded, 1)
        for i in range(cut.folds):
            place = 2 * part + i * group
            out[place : place + group] = folded[:, i * 128 : (i + 1) * 128]
        if d == side:
            out[cut.length : cut.length + D] = y[2 * part :, 128 * side : 128 * side + 128]
            out[cut.length + D :] = jnp.concatenate([spare[2 * part :], jnp.zeros((D, 64), F32)], 1)


def pack(d, measured, mask, cut):
    shapes = [jax.ShapeDtypeStruct((cut.length + (2 * cut.D if d == side else 0), 128), F32) for side in range(2)]
    scratch = [
        pltpu.VMEM((cut.ch, cut.S, cut.D, cut.W), F32),
        pltpu.VMEM((cut.S, cut.D, cut.W), jnp.int32),
        pltpu.SemaphoreType.DMA((2,)),
    ]
    body = functools.partial(pack_kernel, cut, d)
    return call(body, "pack", (measured, mask), shapes, scratch, far=(0, 1), space=HBM, limit=PACK)


def fold_kernel(kernel, out):
    count = out.shape[0]
    half = kernel.shape[1] // 2
    some = kernel[pl.ds(lax.axis_index("kx") * count, count)]
    out[...] = jnp.concatenate([some[:, :half], some[:, half:]], -1)


def fold(kernel):
    count, coils, inputs = kernel.shape
    shape = jax.ShapeDtypeStruct((count // 2, coils // 2, 2 * inputs), F32)
    return call(fold_kernel, "fold", (kernel,), [shape])[0]


def weights_kernel(cut, own, *refs):
    folded, (single, double, kernel) = refs[:-3], refs[-3:]
    count, coils, inputs = kernel.shape
    local = coils // cut.C
    c, x = lax.axis_index("coil"), lax.axis_index("kx")
    kernel[:, pl.ds(pl.multiple_of(c * local, local), local)] = own[...]
    for i, half in enumerate(folded):
        d, other = i // 2 + 1, i % 2
        place = pl.multiple_of(lax.bitwise_xor(c, d) * local, local)
        taps = pl.ds(lax.bitwise_xor(x, other) * (count // 2), count // 2)
        kernel[taps, pl.ds(place, local // 2)] = half[..., :inputs]
        kernel[taps, pl.ds(place + local // 2, local // 2)] = half[..., inputs:]

    def parts(tap):
        re, im = kernel[2 * tap], kernel[2 * tap + 1]
        return re[:, :coils], im[:, :coils], re[:, coils:], im[:, coils:]

    N = 4 * coils
    taps = count // 2
    for t in range(taps):
        pr, pi, vr, vi = parts(t)
        qr, qi, ur, ui = parts(taps - 1 - t)
        block = jnp.concatenate(
            [
                jnp.concatenate([pr, -pi, vr, vi], 1),
                jnp.concatenate([pi, pr, vi, -vr], 1),
                jnp.concatenate([ur, ui, qr, -qi], 1),
                jnp.concatenate([ui, -ur, qi, qr], 1),
            ],
            0,
        ).T
        hi, lo = split(block)
        e, tap = t % 3, t // 3
        single[tap, :, e * N : (e + 1) * N] = hi
        double[tap, :, 2 * e * N : (2 * e + 1) * N] = hi
        double[tap, :, (2 * e + 1) * N : (2 * e + 2) * N] = lo


def build_weights(kernel, folded, cut):
    count, coils, inputs = kernel.shape
    N = cut.channels
    shapes = [jax.ShapeDtypeStruct((9, N, 3 * N), BF16), jax.ShapeDtypeStruct((9, N, 6 * N), BF16)]
    scratch = [pltpu.VMEM((count, coils * cut.C, inputs), F32)]
    return call(functools.partial(weights_kernel, cut), "weights", (kernel, *folded), shapes, scratch, cost=LITTLE)


def spread(cut, target, k, first, rest):
    D, H, S = cut.D, cut.H, cut.S
    if k == 0:
        for r in (0, 1, S + 2, S + 3):
            target[r] = jnp.zeros(target.shape[1:], F32)
    for r in range(cut.base):
        target[r + 2, pl.ds(k, H, stride=D)] = first[r * H : (r + 1) * H]
    for r in range(cut.base, S):
        target[r + 2, pl.ds(k, H, stride=D)] = rest[(r - cut.base) * H : (r - cut.base + 1) * H]
    for r in range(S):
        place = cut.spare + 2 * r
        target[r + 2, pl.ds(H * D + k, 2, stride=D)] = rest[place : place + 2]


def assemble(cut, side, msgs, x, main, spare):
    D, half, part = cut.D, cut.half, cut.part
    for d, msg in enumerate(msgs):
        other = lax.bitwise_xor(lax.axis_index("coil"), d)
        folded = msg[2 * part : cut.length].reshape(cut.folds, cut.group, 128)
        folded = jnp.concatenate([folded[i] for i in range(cut.folds)], 1)
        for ri in range(2):
            start = pl.multiple_of((ri * cut.C + other) * part, part)
            main[pl.ds(start, part)] = msg[ri * part : (ri + 1) * part]
        for i in range(16):
            start = pl.multiple_of((i // 8 * cut.C + other) * part + i % 8 * cut.group, cut.group)
            spare[pl.ds(start, cut.group), : cut.used] = folded[:, i * cut.used : (i + 1) * cut.used]
    gap = jnp.zeros((half, 128), F32)
    for k in range(D):
        some = pl.ds(D - 1 - k if side else k, half, stride=D)
        blocks = [jnp.concatenate([gap, v] if side else [v, gap], 0).T for v in (main[some], spare[some])]
        spread(cut, x, k, *blocks)


def physical_kernel(cut, ready, *refs):
    msgs, (x, main, spare) = refs[: cut.C], refs[cut.C :]
    assemble(cut, 0, msgs, x, main, spare)


def mirrored_kernel(cut, physical, marks, *refs):
    msgs, (x, rows, main, spare) = refs[: cut.C], refs[-4:]
    assemble(cut, 1, msgs, x, main, spare)
    x[...] = x[...] + physical[...]
    lower, S = lax.axis_index("kx") == 0, cut.S
    rows[0] = jnp.where(lower, x[S + 1], x[2])
    rows[1] = jnp.where(lower, x[S], x[3])
    rows[2] = jnp.where(lower, marks[S + 1], marks[2])


def marks_kernel(cut, ready, own, other, marks):
    D, half = cut.D, cut.half
    lane = lax.broadcasted_iota(jnp.int32, (128, cut.channels), 1)
    flags = [msg[cut.length : cut.length + 2 * D] for msg in (own, other)]
    flags = jnp.concatenate(flags + [jnp.zeros((128 - 4 * D, 128), F32)], 0).T
    for k in range(D):
        j = D - 1 - k
        first = jnp.where(lane < half, flags[:, k : k + 1], flags[:, 2 * D + j : 2 * D + j + 1])
        rest = jnp.where(lane < half, flags[:, D + k : D + k + 1], flags[:, 3 * D + j : 3 * D + j + 1])
        spread(cut, marks, k, first, rest)


def points(cut, weights, msgs):
    row = (cut.V * cut.D, cut.channels)
    window = jax.ShapeDtypeStruct((cut.S + 4, *row), F32)
    stages = [pltpu.VMEM((cut.half * cut.D, 128), F32)] * 2
    args = (weights[0], *msgs[0::2])
    (x,) = call(functools.partial(physical_kernel, cut), "physical", args, [window], stages, far=(0,), cost=LITTLE)
    added = inside_half(0, x, weights, cut)
    flags = (added, msgs[0], msgs[3])
    (marks,) = call(functools.partial(marks_kernel, cut), "marks", flags, [window], far=(0,), cost=LITTLE)
    args = (x, marks, *msgs[1::2])
    x, rows = call(
        functools.partial(mirrored_kernel, cut),
        "mirrored",
        args,
        [window, jax.ShapeDtypeStruct((3, *row), F32)],
        stages,
    )
    return x, marks, rows, added


def edges(cut):
    _, c, x = place()
    inner = c == cut.C - 1
    return jnp.logical_and(inner, x == 1), jnp.logical_and(inner, x == 0)


def put_faces(cut, slot, row, face_a, face_b):
    D, V = cut.D, cut.V
    odd = lax.rem(lax.axis_index("kz"), 2) == 1
    first, final = row(pl.ds(0, V, stride=D)), row(pl.ds(D - 1, V, stride=D))
    face_a[slot * V : (slot + 1) * V] = jnp.where(odd, first, final)
    face_b[slot * V : (slot + 1) * V] = jnp.where(odd, final, first)


def faces_kernel(cut, x, rows, face_a, face_b):
    own, G = cut.own(), cut.G
    before, after = edges(cut)
    other = {0: (before, 1), 1: (before, 0), G + 2: (after, 0), G + 3: (after, 1)}
    for slot in range(G + 4):

        def row(some):
            value = x[own + slot, some]
            if slot in other:
                there, which = other[slot]
                value = jnp.where(there, rows[which, some], value)
            return value

        put_faces(cut, slot, row, face_a, face_b)


def faces(x, rows, cut):
    face = jax.ShapeDtypeStruct(((cut.G + 4) * cut.V, cut.channels), F32)
    return call(functools.partial(faces_kernel, cut), "faces", (x, rows), [face, face])


def multiply(hi, lo, single, double):
    N = single.shape[-1]
    groups = double.shape[-1] // (2 * 128)
    y, z = dot(hi, double), dot(lo, single)
    N = N // groups
    return [
        y[:, 2 * e * N : (2 * e + 1) * N] + y[:, (2 * e + 1) * N : (2 * e + 2) * N] + z[:, e * N : (e + 1) * N]
        for e in range(groups)
    ]


def shifted(y, D):
    M = y[0].shape[0]
    rows = lax.broadcasted_iota(jnp.int32, y[0].shape, 0) % D
    later = jnp.where(rows == 0, 0.0, pltpu.roll(y[0], 1, 0))
    sooner = jnp.where(rows == D - 1, 0.0, pltpu.roll(y[2], M - 1, 0))
    return y[1] + later + sooner


def inside_kernel(cut, x, single, double, out, hi, lo):
    D = cut.D
    count, L, channels = out.shape
    gap = jnp.zeros((D, channels), F32)
    for slot in range(count + 2):
        row = x[slot]
        high = row.astype(BF16).astype(F32)
        for ref, value in ((hi, high), (lo, row - high)):
            ref[0, slot] = jnp.concatenate([gap, value[:-D]], 0).astype(BF16)
            ref[1, slot] = value.astype(BF16)
            ref[2, slot] = jnp.concatenate([value[D:], gap], 0).astype(BF16)

    def window(ref):
        return jnp.concatenate(
            [jnp.concatenate([ref[b, i + a, :L] for i in range(count)], 0) for a in range(3) for b in range(3)], 1
        )

    K = 9 * channels
    y = multiply(window(hi), window(lo), single[...].reshape(K, -1), double[...].reshape(K, -1))
    out[...] = shifted(y, D).reshape(count, L, channels)


def inside(x, weights, cut):
    out = jax.ShapeDtypeStruct((cut.G, cut.H * cut.D, cut.channels), F32)
    scratch = [pltpu.VMEM((3, cut.G + 2, cut.V * cut.D, cut.channels), BF16)] * 2
    return call(functools.partial(inside_kernel, cut), "inside", (x, *weights), [out], scratch)[0]


def half_weights(weights, side, half):
    rows = slice(half, 2 * half) if side else slice(0, half)
    order = [0, 1, 3, 4, 6, 7, 2, 5, 8]
    picked = [weights[tap, rows] for tap in order]
    return jnp.concatenate(picked + [jnp.zeros_like(picked[0])], 0)


def inside_half_kernel(cut, side, x, *refs):
    if side:
        rows, added, single, double, out, hi, lo = refs
    else:
        single, double, out, hi, lo = refs
    D, half, own = cut.D, cut.half, cut.own()
    count, L, channels = out.shape
    gap = jnp.zeros((D, channels), F32)
    left = lax.broadcasted_iota(jnp.int32, (L, channels), 1) < half

    def pair(one, two):
        return jnp.where(left, one[side], two[1 - side])

    none = (jnp.zeros((L, channels), F32),) * 2

    def versions(slot):
        if slot == count + 2:
            return none, none, none
        row = x[own + slot]
        both = (row, pltpu.roll(row, half, 1))
        sooner = tuple(jnp.concatenate([gap, v[:-D]], 0) for v in both)
        later = tuple(jnp.concatenate([v[D:], gap], 0) for v in both)
        return sooner, both, later

    following = versions(0)
    for slot in range(count + 2):
        now, following = following, versions(slot + 1)
        for i, value in enumerate((pair(now[0], now[1]), pair(now[2], following[2]))):
            hi[i, slot], lo[i, slot] = split(value)

    def window(ref):
        columns = [(0, 0), (0, 1), (0, 2), (1, 0), (1, 2)]
        return jnp.concatenate(
            [jnp.concatenate([ref[i, j + a] for j in range(count)], 0) for i, a in columns], 1
        )

    y = multiply(window(hi), window(lo), *(half_weights(w, side, half) for w in (single, double)))
    y = shifted(y, D).reshape(count, L, channels)
    if not side:
        out[...] = y
        return
    out[...] = y + added[...]
    before, after = edges(cut)
    lower = lax.axis_index("kx") == 0
    pieces = []
    for row in (rows[0], rows[1]):
        parts = [split(v) for v in (jnp.concatenate([gap, row[:-D]], 0), row, jnp.concatenate([row[D:], gap], 0))]
        pieces.append([jnp.concatenate([p[i] for p in parts], 1) for i in range(2)])
    near, second = pieces
    wide = [
        jnp.concatenate([jnp.concatenate([n, f], 1), jnp.concatenate([jnp.zeros_like(n), n], 1)], 0)
        for n, f in zip(near, second)
    ]
    outer = pl.ds(jnp.where(lower, 6, 0), 3)
    taps = [jnp.concatenate([w[3:6], w[outer]], 0).reshape(6 * channels, -1) for w in (single, double)]
    y = shifted(multiply(*wide, *taps), D)
    there = jnp.logical_or(before, after)
    for i in range(2):
        target = jnp.where(lower, count - 1 - i, i)
        out[target] += jnp.where(there, y[i * L : (i + 1) * L], 0.0)


def inside_half(side, x, weights, cut, *more):
    count, L = cut.G + 2, cut.V * cut.D
    out = jax.ShapeDtypeStruct((count, L, cut.channels), F32)
    scratch = [pltpu.VMEM((2, count + 2, L, cut.channels), BF16)] * 2
    body = functools.partial(inside_half_kernel, cut, side)
    cost = None if side else LITTLE
    return call(body, "inside_mirrored" if side else "inside_physical", (x, *more, *weights), [out], scratch, cost=cost)[0]


def add_planes(cut, width, target, got_a, got_b, single, double, planes):
    D, V, pitch = cut.D, cut.V, cut.pitch
    z, Z = lax.axis_index("kz"), lax.axis_size("kz")
    odd = lax.rem(z, 2) == 1
    ends = jnp.logical_or(z == 0, z == Z - 1)
    count = target.shape[0]
    height = -(-count * pitch // 16) * 16
    N, K = cut.channels, 9 * cut.channels
    got_a, got_b = got_a[...], jnp.where(ends, 0.0, got_b[...])
    for e, k, plane in ((0, 0, jnp.where(odd, got_a, got_b)), (2, D - 1, jnp.where(odd, got_b, got_a))):
        planes[...] = jnp.zeros_like(planes)
        for slot in range(count + 2):
            column = plane[slot * V : (slot + 1) * V]
            for b in range(3):
                place = 8 + slot * pitch + 1 - b
                planes[b, place : place + V] = column
        parts = [
            split(planes[b, 8 + a * pitch : 8 + a * pitch + height])
            for a in range(3)
            for b in range(3)
        ]
        hi, lo = (jnp.concatenate([part[i] for part in parts], 1) for i in range(2))
        one = single[:, :, e * N : (e + 1) * N].reshape(K, N)
        two = double[:, :, 2 * e * N : (2 * e + 2) * N].reshape(K, 2 * N)
        (y,) = multiply(hi, lo, one, two)
        for i in range(count):
            target[i, pl.ds(k, width, stride=D)] += y[i * pitch : i * pitch + width]


def planes_scratch(cut, count):
    return pltpu.VMEM((3, 8 + (count + 2) * cut.pitch + 16, cut.channels), F32)


def middle_kernel(cut, x, marks, rows, main, got_a, got_b, single, double, out, face_a, face_b, planes):
    G, own = cut.G, cut.own()
    before, after = edges(cut)
    core, piece = lax.axis_index("kx"), cut.piece()
    out[...] = main[...]
    add_planes(cut, cut.V, out, got_a, got_b, single, double, planes)
    first = jnp.logical_and(core == 0, piece == 0)
    final = jnp.logical_and(core == 1, piece == cut.C - 1)
    for i in range(G + 2):
        kept, mark = x[own + 1 + i], marks[own + 1 + i]
        if i in (0, G + 1):
            there, outside = (before, first) if i == 0 else (after, final)
            kept, mark = jnp.where(there, rows[0], kept), jnp.where(there, rows[2], mark)
            value = jnp.where(outside, 0.0, jnp.where(mark > 0.5, kept, out[i]))
        else:
            value = jnp.where(mark > 0.5, kept, out[i])
        out[i] = value
        put_faces(cut, i, lambda some: out[i, some], face_a, face_b)


def last_kernel(cut, main, got_b, got_a, single, double, *rest):
    C, D, H, G, half = cut.C, cut.D, cut.H, cut.G, cut.half
    outs, (y, stage, planes) = rest[: 2 * C], rest[2 * C :]
    y[...] = main[...]
    add_planes(cut, H, y, got_a, got_b, single, double, planes)
    flip = reversal(G * H)
    for k in range(D):
        rows = y[:, pl.ds(k, H, stride=D)].reshape(G * H, 2 * half).T
        stage[pl.ds(k, half, stride=D)] = rows[:half]
        hi, lo = split(rows[half:])
        stage[pl.ds(half * D + D - 1 - k, half, stride=D)] = dot(hi, flip) + dot(lo, flip)
    for d in range(C):
        for side in range(2):
            for ri in range(2):
                start = ((side * 2 + ri) * C + lax.bitwise_xor(lax.axis_index("coil"), d)) * cut.part
                start = pl.multiple_of(start, cut.part)
                outs[2 * d + side][ri * cut.part : (ri + 1) * cut.part] = stage[pl.ds(start, cut.part)]


def unpack_kernel(cut, d, measured, mask, mirrored, own, *refs):
    out, rows, sems = refs[-3:]
    ch, D, G, H = cut.ch, cut.D, cut.G, cut.H
    start = cut.piece(d) * G
    own, mirrored = (msg[...].reshape(ch, D, G * H) for msg in (own, mirrored))
    copies = []
    for j in range(G):
        sampled = (mask[start + j] == 1)[None]
        value = jnp.concatenate([msg[:, :, j * H : (j + 1) * H] for msg in (own, mirrored)], -1)
        rows[:, j] = jnp.where(sampled, measured[:, start + j], value)
        if j % 2:
            some = pl.ds(j - 1, 2)
            copy = pltpu.make_async_copy(rows.at[:, some], out.at[:, pl.ds(start + j - 1, 2)], sems.at[j // 2])
            copy.start()
            copies.append(copy)
    for copy in copies:
        copy.wait()


def unpack(d, measured, mask, msgs, cut, into=None):
    args = (measured, mask, *msgs) + (() if into is None else (into,))
    (out,) = call(
        functools.partial(unpack_kernel, cut, d),
        "unpack",
        args,
        [jax.ShapeDtypeStruct(measured.shape, F32)],
        [pltpu.VMEM((cut.ch, cut.G, cut.D, cut.W), F32), pltpu.SemaphoreType.DMA((cut.G // 2,))],
        far=() if into is None else (len(args) - 1,),
        out=ANY,
        input_output_aliases={} if into is None else {len(args) - 1: 0},
    )
    return out


def on_device(measured, mask, kernel):
    Z, C, X = (lax.axis_size(axis) for axis in AXES)
    every = [(z, c, x) for z in range(Z) for c in range(C) for x in range(X)]

    def index(z, c, x):
        return (z * C + c) * X + x

    def send(array, target):
        return lax.ppermute(array, AXES, [(index(*p), index(*target(*p))) for p in every])

    def exchange(msgs):
        got = list(msgs)
        for d in range(C):
            got[2 * d + 1] = send(msgs[2 * d + 1], lambda z, c, x: (Z - 1 - z, c ^ d, X - 1 - x))
        for d in range(1, C):
            got[2 * d] = send(msgs[2 * d], lambda z, c, x: (z, c ^ d, x))
        return got

    def plane_a(z, c, x):
        return (z ^ 1, c, x)

    def plane_b(z, c, x):
        other = z + 1 if z % 2 else z - 1
        return (other, c, x) if 0 <= other < Z else (z, c, X - 1 - x)

    def core(z, c, x):
        return (z, c, X - 1 - x)

    parts, coils, rows, D, W = measured.shape
    cut = Cut(rows, D, W, C, 2 * parts * coils * C)
    flat = measured.reshape(parts * coils, rows, D, W)
    kernel = kernel.reshape(-1, *kernel.shape[2:])
    msgs = []
    for d in reversed(range(C)):
        msgs = [*pack(d, flat, mask, cut), *msgs]
        kernel, mask, *msgs = lax.optimization_barrier((kernel, mask, *msgs)) if d else (kernel, mask, *msgs)
    msgs = exchange(msgs)
    folded = []
    for d in range(1, C):
        half = send(fold(kernel), lambda z, c, x: (z, c ^ d, x))
        folded += [half, send(half, core)]
    weights = build_weights(kernel, folded, cut)
    state, marks, near, added = points(cut, weights, msgs)
    near = send(near, core)
    got = [send(face, to) for face, to in zip(faces(state, near, cut), (plane_a, plane_b))]
    main = inside_half(1, state, weights, cut, near, added)
    face = jax.ShapeDtypeStruct(((cut.G + 2) * cut.V, cut.channels), F32)
    state, *sides = call(
        functools.partial(middle_kernel, cut),
        "middle",
        (state, marks, near, main, *got, *weights),
        [jax.ShapeDtypeStruct(main.shape, F32), face, face],
        [planes_scratch(cut, cut.G + 2)],
    )
    got = [send(face, to) for face, to in zip(sides[::-1], (plane_b, plane_a))]
    main = inside(state, weights, cut)
    message = jax.ShapeDtypeStruct((cut.ch * D, cut.G * cut.H), F32)
    msgs = call(
        functools.partial(last_kernel, cut),
        "last",
        (main, *got, *weights),
        [message] * (2 * C),
        [pltpu.VMEM(main.shape, F32), pltpu.VMEM((cut.channels * D, cut.G * cut.H), F32), planes_scratch(cut, cut.G)],
    )
    msgs = exchange(msgs)
    out = None
    for d in reversed(range(C)):
        out = unpack(d, flat, mask, (msgs[2 * d + 1], msgs[2 * d]), cut, out)
    return out.reshape(measured.shape)


def solution(mesh):
    placed = (
        P(None, ("grp", "coil"), "kx", "kz", None),
        P(("grp", "kx"), "kz", None),
        P(None, None, "coil", None),
    )
    return jax.shard_map(
        on_device,
        mesh=mesh,
        in_specs=placed,
        out_specs=P(None, ("grp", "coil"), "kx", "kz", None),
        check_vma=False,
    )
```

```python
import functools

import jax
import jax.numpy as jnp
from jax import lax
from jax.experimental import pallas as pl
from jax.experimental.pallas import tpu as pltpu
from jax.sharding import PartitionSpec as P

PACK = 56 << 20
LITTLE = pl.CostEstimate(flops=1000, bytes_accessed=1000, transcendentals=0)
AXES = ("kz", "coil", "kx")
F32 = jnp.float32
BF16 = jnp.bfloat16
ANY = pl.BlockSpec(memory_space=pl.ANY)
HBM = pl.BlockSpec(memory_space=pltpu.HBM)
VMEM = pl.BlockSpec(memory_space=pltpu.VMEM)


def call(body, name, args, shapes, scratch=(), far=(), space=ANY, out=VMEM, limit=32 << 20, cost=None, **options):
    return pl.pallas_call(
        body,
        out_shape=shapes,
        in_specs=[space if i in far else VMEM for i in range(len(args))],
        out_specs=[out] * len(shapes),
        scratch_shapes=list(scratch),
        compiler_params=pltpu.CompilerParams(vmem_limit_bytes=limit),
        cost_estimate=cost,
        name=name,
        **options,
    )(*args)


def split(x):
    hi = x.astype(BF16)
    return hi, (x - hi.astype(F32)).astype(BF16)


def reversal(n):
    row = lax.broadcasted_iota(jnp.int32, (n, n), 0)
    column = lax.broadcasted_iota(jnp.int32, (n, n), 1)
    return jnp.where(row + column == n - 1, 1.0, 0.0).astype(BF16)


def dot(a, b):
    return jnp.dot(a, b, preferred_element_type=F32)


class Cut:
    def __init__(self, rows, D, W, C, channels):
        self.rows, self.D, self.W, self.C = rows, D, W, C
        self.channels = channels
        self.half = channels // 2
        self.ch = self.half // C
        self.G = rows // C
        self.S = min(rows, self.G + (2 if C == 2 else 4))
        self.H = W // 2
        self.V = self.H + 2
        self.base = 128 // self.H
        self.spare = (self.S - self.base) * self.H
        self.part = self.ch // 2 * D
        self.used = self.spare + 2 * self.S
        self.group = self.ch * D // 16
        self.folds = -(-16 * self.used // 128)
        self.length = 2 * self.part + self.folds * self.group
        self.pitch = -(-(self.V + 1) // 8) * 8

    def piece(self, d=0):
        c, x = lax.bitwise_xor(lax.axis_index("coil"), d), lax.axis_index("kx")
        return jnp.where(x == 0, c, self.C - 1 - c)

    def start(self, d=0):
        return jnp.clip(self.G * self.piece(d) - 2, 0, self.rows - self.S)

    def own(self):
        return self.G * self.piece() - self.start()


def place():
    return tuple(lax.axis_index(axis) for axis in AXES)


def arrangement(cut):
    S, H, W = cut.S, cut.H, cut.W
    shift = H.bit_length() - 1
    j = lax.broadcasted_iota(jnp.int32, (1, 384), 1)
    own = j - jnp.where(j >= 320, 320, jnp.where(j >= 256, 256, jnp.where(j >= 128, 128, 0)))
    spare = j >= 256
    row = lax.shift_right_logical(own, shift)
    main = row * W + lax.bitwise_and(own, H - 1)
    rest = own - cut.spare
    edge = lax.shift_right_logical(rest, 1) * W + H + lax.bitwise_and(rest, 1)
    source = jnp.where(spare, jnp.where(own < cut.spare, main + cut.base * W, edge), main)
    mirrored = jnp.logical_or(jnp.logical_and(j >= 128, j < 256), j >= 320)
    source = jnp.where(mirrored, S * W - 1 - source, source)
    source = jnp.where(jnp.logical_and(spare, rest >= 2 * S), -1, source)
    lane = lax.broadcasted_iota(jnp.int32, (S * W, 384), 0)
    return jnp.where(lane == source, 1.0, 0.0).astype(BF16)


def pack_kernel(cut, d, measured, mask, *refs):
    S, ch, D, W, part = cut.S, cut.ch, cut.D, cut.W, cut.part
    outs, (rows, marks, sems) = refs[:2], refs[2:]
    start = cut.start(d)
    copies = [pltpu.make_async_copy(mask.at[pl.ds(start, S)], marks, sems.at[0])]
    copies.append(pltpu.make_async_copy(measured.at[:, pl.ds(start, S)], rows, sems.at[1]))
    for copy in copies:
        copy.start()
    order = arrangement(cut)
    for copy in copies:
        copy.wait()
    sampled = [marks[j] == 1 for j in range(S)]
    kept = [jnp.where(sampled[j][None], rows[:, j], 0.0) for j in range(S)]
    kept = jnp.concatenate(kept, -1).reshape(ch * D, S * W)
    if d < 2:
        kept = jnp.concatenate([kept, jnp.concatenate([jnp.where(s, 1.0, 0.0) for s in sampled], -1)], 0)
    hi, lo = split(kept)
    y = dot(hi, order) + dot(lo, order)
    for side in (1, 0):
        out = outs[side]
        out[: 2 * part] = y[: 2 * part, 128 * side : 128 * side + 128]
        spare = y[:, 256 + 64 * side : 320 + 64 * side]
        group = cut.group
        folded = [spare[i * group : (i + 1) * group, : cut.used] for i in range(16)]
        if cut.folds * 128 > 16 * cut.used:
            folded.append(jnp.zeros((group, cut.folds * 128 - 16 * cut.used), F32))
        folded = jnp.concatenate(folded, 1)
        for i in range(cut.folds):
            place = 2 * part + i * group
            out[place : place + group] = folded[:, i * 128 : (i + 1) * 128]
        if d == side:
            out[cut.length : cut.length + D] = y[2 * part :, 128 * side : 128 * side + 128]
            out[cut.length + D :] = jnp.concatenate([spare[2 * part :], jnp.zeros((D, 64), F32)], 1)


def pack(d, measured, mask, cut):
    shapes = [jax.ShapeDtypeStruct((cut.length + (2 * cut.D if d == side else 0), 128), F32) for side in range(2)]
    scratch = [
        pltpu.VMEM((cut.ch, cut.S, cut.D, cut.W), F32),
        pltpu.VMEM((cut.S, cut.D, cut.W), jnp.int32),
        pltpu.SemaphoreType.DMA((2,)),
    ]
    body = functools.partial(pack_kernel, cut, d)
    return call(body, "pack", (measured, mask), shapes, scratch, far=(0, 1), space=HBM, limit=PACK if d else 52 << 20)


def fold_kernel(kernel, out):
    count = out.shape[0]
    half = kernel.shape[1] // 2
    some = kernel[pl.ds(lax.axis_index("kx") * count, count)]
    out[...] = jnp.concatenate([some[:, :half], some[:, half:]], -1)


def fold(kernel):
    count, coils, inputs = kernel.shape
    shape = jax.ShapeDtypeStruct((count // 2, coils // 2, 2 * inputs), F32)
    return call(fold_kernel, "fold", (kernel,), [shape])[0]


def weights_kernel(cut, own, *refs):
    folded, (single, double, kernel) = refs[:-3], refs[-3:]
    count, coils, inputs = kernel.shape
    local = coils // cut.C
    c, x = lax.axis_index("coil"), lax.axis_index("kx")
    kernel[:, pl.ds(pl.multiple_of(c * local, local), local)] = own[...]
    for i, half in enumerate(folded):
        d, other = i // 2 + 1, i % 2
        place = pl.multiple_of(lax.bitwise_xor(c, d) * local, local)
        taps = pl.ds(lax.bitwise_xor(x, other) * (count // 2), count // 2)
        kernel[taps, pl.ds(place, local // 2)] = half[..., :inputs]
        kernel[taps, pl.ds(place + local // 2, local // 2)] = half[..., inputs:]

    def parts(tap):
        re, im = kernel[2 * tap], kernel[2 * tap + 1]
        return re[:, :coils], im[:, :coils], re[:, coils:], im[:, coils:]

    N = 4 * coils
    taps = count // 2
    for t in range(taps):
        pr, pi, vr, vi = parts(t)
        qr, qi, ur, ui = parts(taps - 1 - t)
        block = jnp.concatenate(
            [
                jnp.concatenate([pr, -pi, vr, vi], 1),
                jnp.concatenate([pi, pr, vi, -vr], 1),
                jnp.concatenate([ur, ui, qr, -qi], 1),
                jnp.concatenate([ui, -ur, qi, qr], 1),
            ],
            0,
        ).T
        hi, lo = split(block)
        e, tap = t % 3, t // 3
        single[tap, :, e * N : (e + 1) * N] = hi
        double[tap, :, 2 * e * N : (2 * e + 1) * N] = hi
        double[tap, :, (2 * e + 1) * N : (2 * e + 2) * N] = lo


def build_weights(kernel, folded, cut):
    count, coils, inputs = kernel.shape
    N = cut.channels
    shapes = [jax.ShapeDtypeStruct((9, N, 3 * N), BF16), jax.ShapeDtypeStruct((9, N, 6 * N), BF16)]
    scratch = [pltpu.VMEM((count, coils * cut.C, inputs), F32)]
    return call(functools.partial(weights_kernel, cut), "weights", (kernel, *folded), shapes, scratch, cost=LITTLE)


def spread(cut, target, k, first, rest):
    D, H, S = cut.D, cut.H, cut.S
    if k == 0:
        for r in (0, 1, S + 2, S + 3):
            target[r] = jnp.zeros(target.shape[1:], F32)
    for r in range(cut.base):
        target[r + 2, pl.ds(k, H, stride=D)] = first[r * H : (r + 1) * H]
    for r in range(cut.base, S):
        target[r + 2, pl.ds(k, H, stride=D)] = rest[(r - cut.base) * H : (r - cut.base + 1) * H]
    for r in range(S):
        place = cut.spare + 2 * r
        target[r + 2, pl.ds(H * D + k, 2, stride=D)] = rest[place : place + 2]


def assemble(cut, side, msgs, x, main, spare):
    D, half, part = cut.D, cut.half, cut.part
    for d, msg in enumerate(msgs):
        other = lax.bitwise_xor(lax.axis_index("coil"), d)
        folded = msg[2 * part : cut.length].reshape(cut.folds, cut.group, 128)
        folded = jnp.concatenate([folded[i] for i in range(cut.folds)], 1)
        for ri in range(2):
            start = pl.multiple_of((ri * cut.C + other) * part, part)
            main[pl.ds(start, part)] = msg[ri * part : (ri + 1) * part]
        for i in range(16):
            start = pl.multiple_of((i // 8 * cut.C + other) * part + i % 8 * cut.group, cut.group)
            spare[pl.ds(start, cut.group), : cut.used] = folded[:, i * cut.used : (i + 1) * cut.used]
    gap = jnp.zeros((half, 128), F32)
    for k in range(D):
        some = pl.ds(D - 1 - k if side else k, half, stride=D)
        blocks = [jnp.concatenate([gap, v] if side else [v, gap], 0).T for v in (main[some], spare[some])]
        spread(cut, x, k, *blocks)


def physical_kernel(cut, ready, *refs):
    msgs, (x, main, spare) = refs[: cut.C], refs[cut.C :]
    assemble(cut, 0, msgs, x, main, spare)


def mirrored_kernel(cut, physical, ready, *refs):
    msgs, (x, rows, main, spare) = refs[: cut.C], refs[-4:]
    assemble(cut, 1, msgs, x, main, spare)
    x[...] = x[...] + physical[...]
    lower, S = lax.axis_index("kx") == 0, cut.S
    rows[0] = jnp.where(lower, x[S + 1], x[2])
    rows[1] = jnp.where(lower, x[S], x[3])


def marks_kernel(cut, ready, own, other, marks, edge):
    D, half = cut.D, cut.half
    lane = lax.broadcasted_iota(jnp.int32, (128, cut.channels), 1)
    flags = [msg[cut.length : cut.length + 2 * D] for msg in (own, other)]
    flags = jnp.concatenate(flags + [jnp.zeros((128 - 4 * D, 128), F32)], 0).T
    for k in range(D):
        j = D - 1 - k
        first = jnp.where(lane < half, flags[:, k : k + 1], flags[:, 2 * D + j : 2 * D + j + 1])
        rest = jnp.where(lane < half, flags[:, D + k : D + k + 1], flags[:, 3 * D + j : 3 * D + j + 1])
        spread(cut, marks, k, first, rest)
    edge[...] = jnp.where(lax.axis_index("kx") == 0, marks[cut.S + 1], marks[2])


def points(cut, weights, msgs, swap):
    row = (cut.V * cut.D, cut.channels)
    window = jax.ShapeDtypeStruct((cut.S + 4, *row), F32)
    stages = [pltpu.VMEM((cut.half * cut.D, 128), F32)] * 2
    args = (weights[0], *msgs[0::2])
    (x,) = call(functools.partial(physical_kernel, cut), "physical", args, [window], stages, far=(0,), cost=LITTLE)
    added = inside_half(0, x, weights, cut)
    flags = (added, msgs[0], msgs[3])
    edge = jax.ShapeDtypeStruct(row, F32)
    marks, edge = call(functools.partial(marks_kernel, cut), "marks", flags, [window, edge], far=(0,), cost=LITTLE)
    edge = swap(edge)
    args = (x, edge, *msgs[1::2])
    x, rows = call(
        functools.partial(mirrored_kernel, cut),
        "mirrored",
        args,
        [window, jax.ShapeDtypeStruct((2, *row), F32)],
        stages,
        far=(1,),
    )
    return x, marks, edge, rows, added


def edges(cut):
    _, c, x = place()
    inner = c == cut.C - 1
    return jnp.logical_and(inner, x == 1), jnp.logical_and(inner, x == 0)


def put_faces(cut, slot, row, face_a, face_b):
    D, V = cut.D, cut.V
    odd = lax.rem(lax.axis_index("kz"), 2) == 1
    first, final = row(pl.ds(0, V, stride=D)), row(pl.ds(D - 1, V, stride=D))
    face_a[slot * V : (slot + 1) * V] = jnp.where(odd, first, final)
    face_b[slot * V : (slot + 1) * V] = jnp.where(odd, final, first)


def faces_kernel(cut, x, rows, face_a, face_b):
    own, G = cut.own(), cut.G
    before, after = edges(cut)
    other = {0: (before, 1), 1: (before, 0), G + 2: (after, 0), G + 3: (after, 1)}
    for slot in range(G + 4):

        def row(some):
            value = x[own + slot, some]
            if slot in other:
                there, which = other[slot]
                value = jnp.where(there, rows[which, some], value)
            return value

        put_faces(cut, slot, row, face_a, face_b)


def faces(x, rows, cut):
    face = jax.ShapeDtypeStruct(((cut.G + 4) * cut.V, cut.channels), F32)
    return call(functools.partial(faces_kernel, cut), "faces", (x, rows), [face, face])


def multiply(hi, lo, single, double):
    N = single.shape[-1]
    groups = double.shape[-1] // (2 * 128)
    y, z = dot(hi, double), dot(lo, single)
    N = N // groups
    return [
        y[:, 2 * e * N : (2 * e + 1) * N] + y[:, (2 * e + 1) * N : (2 * e + 2) * N] + z[:, e * N : (e + 1) * N]
        for e in range(groups)
    ]


def shifted(y, D):
    M = y[0].shape[0]
    rows = lax.broadcasted_iota(jnp.int32, y[0].shape, 0) % D
    later = jnp.where(rows == 0, 0.0, pltpu.roll(y[0], 1, 0))
    sooner = jnp.where(rows == D - 1, 0.0, pltpu.roll(y[2], M - 1, 0))
    return y[1] + later + sooner


def inside_kernel(cut, x, single, double, out, hi, lo):
    D = cut.D
    count, L, channels = out.shape
    gap = jnp.zeros((D, channels), F32)
    for slot in range(count + 2):
        row = x[slot]
        high = row.astype(BF16).astype(F32)
        for ref, value in ((hi, high), (lo, row - high)):
            ref[0, slot] = jnp.concatenate([gap, value[:-D]], 0).astype(BF16)
            ref[1, slot] = value.astype(BF16)
            ref[2, slot] = jnp.concatenate([value[D:], gap], 0).astype(BF16)

    def window(ref):
        return jnp.concatenate(
            [jnp.concatenate([ref[b, i + a, :L] for i in range(count)], 0) for a in range(3) for b in range(3)], 1
        )

    K = 9 * channels
    y = multiply(window(hi), window(lo), single[...].reshape(K, -1), double[...].reshape(K, -1))
    out[...] = shifted(y, D).reshape(count, L, channels)


def inside(x, weights, cut):
    out = jax.ShapeDtypeStruct((cut.G, cut.H * cut.D, cut.channels), F32)
    scratch = [pltpu.VMEM((3, cut.G + 2, cut.V * cut.D, cut.channels), BF16)] * 2
    return call(functools.partial(inside_kernel, cut), "inside", (x, *weights), [out], scratch)[0]


def half_weights(weights, side, half):
    rows = slice(half, 2 * half) if side else slice(0, half)
    order = [0, 1, 3, 4, 6, 7, 2, 5, 8]
    picked = [weights[tap, rows] for tap in order]
    return jnp.concatenate(picked + [jnp.zeros_like(picked[0])], 0)


def inside_half_kernel(cut, side, x, *refs):
    if side:
        rows, added, single, double, out, hi, lo = refs
    else:
        single, double, out, hi, lo = refs
    D, half, own = cut.D, cut.half, cut.own()
    count, L, channels = out.shape
    gap = jnp.zeros((D, channels), F32)
    left = lax.broadcasted_iota(jnp.int32, (L, channels), 1) < half

    def pair(one, two):
        return jnp.where(left, one[side], two[1 - side])

    none = (jnp.zeros((L, channels), F32),) * 2

    def versions(slot):
        if slot == count + 2:
            return none, none, none
        row = x[own + slot]
        both = (row, pltpu.roll(row, half, 1))
        sooner = tuple(jnp.concatenate([gap, v[:-D]], 0) for v in both)
        later = tuple(jnp.concatenate([v[D:], gap], 0) for v in both)
        return sooner, both, later

    following = versions(0)
    for slot in range(count + 2):
        now, following = following, versions(slot + 1)
        for i, value in enumerate((pair(now[0], now[1]), pair(now[2], following[2]))):
            hi[i, slot], lo[i, slot] = split(value)

    def window(ref):
        columns = [(0, 0), (0, 1), (0, 2), (1, 0), (1, 2)]
        return jnp.concatenate(
            [jnp.concatenate([ref[i, j + a] for j in range(count)], 0) for i, a in columns], 1
        )

    y = multiply(window(hi), window(lo), *(half_weights(w, side, half) for w in (single, double)))
    y = shifted(y, D).reshape(count, L, channels)
    if not side:
        out[...] = y
        return
    out[...] = y + added[...]
    before, after = edges(cut)
    lower = lax.axis_index("kx") == 0
    pieces = []
    for row in (rows[0], rows[1]):
        parts = [split(v) for v in (jnp.concatenate([gap, row[:-D]], 0), row, jnp.concatenate([row[D:], gap], 0))]
        pieces.append([jnp.concatenate([p[i] for p in parts], 1) for i in range(2)])
    near, second = pieces
    wide = [
        jnp.concatenate([jnp.concatenate([n, f], 1), jnp.concatenate([jnp.zeros_like(n), n], 1)], 0)
        for n, f in zip(near, second)
    ]
    outer = pl.ds(jnp.where(lower, 6, 0), 3)
    taps = [jnp.concatenate([w[3:6], w[outer]], 0).reshape(6 * channels, -1) for w in (single, double)]
    y = shifted(multiply(*wide, *taps), D)
    there = jnp.logical_or(before, after)
    for i in range(2):
        target = jnp.where(lower, count - 1 - i, i)
        out[target] += jnp.where(there, y[i * L : (i + 1) * L], 0.0)


def inside_half(side, x, weights, cut, *more):
    count, L = cut.G + 2, cut.V * cut.D
    out = jax.ShapeDtypeStruct((count, L, cut.channels), F32)
    scratch = [pltpu.VMEM((2, count + 2, L, cut.channels), BF16)] * 2
    body = functools.partial(inside_half_kernel, cut, side)
    cost = None if side else LITTLE
    return call(body, "inside_mirrored" if side else "inside_physical", (x, *more, *weights), [out], scratch, cost=cost)[0]


def add_planes(cut, width, target, got_a, got_b, single, double, planes):
    D, V, pitch = cut.D, cut.V, cut.pitch
    z, Z = lax.axis_index("kz"), lax.axis_size("kz")
    odd = lax.rem(z, 2) == 1
    ends = jnp.logical_or(z == 0, z == Z - 1)
    count = target.shape[0]
    height = -(-count * pitch // 16) * 16
    N, K = cut.channels, 9 * cut.channels
    got_a, got_b = got_a[...], jnp.where(ends, 0.0, got_b[...])
    planes[...] = jnp.zeros_like(planes)
    for e, k, plane in ((0, 0, jnp.where(odd, got_a, got_b)), (2, D - 1, jnp.where(odd, got_b, got_a))):
        for slot in range(count + 2):
            column = plane[slot * V : (slot + 1) * V]
            for b in range(3):
                place = 8 + slot * pitch + 1 - b
                planes[b, place : place + V] = column
        parts = [
            split(planes[b, 8 + a * pitch : 8 + a * pitch + height])
            for a in range(3)
            for b in range(3)
        ]
        hi, lo = (jnp.concatenate([part[i] for part in parts], 1) for i in range(2))
        one = single[:, :, e * N : (e + 1) * N].reshape(K, N)
        two = double[:, :, 2 * e * N : (2 * e + 2) * N].reshape(K, 2 * N)
        (y,) = multiply(hi, lo, one, two)
        for i in range(count):
            target[i, pl.ds(k, width, stride=D)] += y[i * pitch : i * pitch + width]


def planes_scratch(cut, count):
    return pltpu.VMEM((3, 8 + (count + 2) * cut.pitch + 16, cut.channels), F32)


def middle_kernel(cut, x, marks, edge, rows, main, got_a, got_b, single, double, out, face_a, face_b, planes):
    G, own = cut.G, cut.own()
    before, after = edges(cut)
    core, piece = lax.axis_index("kx"), cut.piece()
    out[...] = main[...]
    add_planes(cut, cut.V, out, got_a, got_b, single, double, planes)
    first = jnp.logical_and(core == 0, piece == 0)
    final = jnp.logical_and(core == 1, piece == cut.C - 1)
    for i in range(G + 2):
        kept, mark = x[own + 1 + i], marks[own + 1 + i]
        if i in (0, G + 1):
            there, outside = (before, first) if i == 0 else (after, final)
            kept, mark = jnp.where(there, rows[0], kept), jnp.where(there, edge[...], mark)
            value = jnp.where(outside, 0.0, jnp.where(mark > 0.5, kept, out[i]))
        else:
            value = jnp.where(mark > 0.5, kept, out[i])
        out[i] = value
        put_faces(cut, i, lambda some: out[i, some], face_a, face_b)


def last_kernel(cut, main, got_b, got_a, single, double, *rest):
    C, D, H, G, half = cut.C, cut.D, cut.H, cut.G, cut.half
    outs, (y, stage, planes) = rest[: 2 * C], rest[2 * C :]
    y[...] = main[...]
    add_planes(cut, H, y, got_a, got_b, single, double, planes)
    flip = reversal(G * H)
    for k in range(D):
        rows = y[:, pl.ds(k, H, stride=D)].reshape(G * H, 2 * half).T
        stage[pl.ds(k, half, stride=D)] = rows[:half]
        hi, lo = split(rows[half:])
        stage[pl.ds(half * D + D - 1 - k, half, stride=D)] = dot(hi, flip) + dot(lo, flip)
    for d in range(C):
        for side in range(2):
            for ri in range(2):
                start = ((side * 2 + ri) * C + lax.bitwise_xor(lax.axis_index("coil"), d)) * cut.part
                start = pl.multiple_of(start, cut.part)
                outs[2 * d + side][ri * cut.part : (ri + 1) * cut.part] = stage[pl.ds(start, cut.part)]


def unpack_kernel(cut, d, measured, mask, mirrored, own, *refs):
    out, rows, sems = refs[-3:]
    ch, D, G, H = cut.ch, cut.D, cut.G, cut.H
    start = cut.piece(d) * G
    own, mirrored = (msg[...].reshape(ch, D, G * H) for msg in (own, mirrored))
    copies = []
    for j in range(G):
        sampled = (mask[start + j] == 1)[None]
        value = jnp.concatenate([msg[:, :, j * H : (j + 1) * H] for msg in (own, mirrored)], -1)
        rows[:, j] = jnp.where(sampled, measured[:, start + j], value)
        if j % 2:
            some = pl.ds(j - 1, 2)
            copy = pltpu.make_async_copy(rows.at[:, some], out.at[:, pl.ds(start + j - 1, 2)], sems.at[j // 2])
            copy.start()
            copies.append(copy)
    for copy in copies:
        copy.wait()


def unpack(d, measured, mask, msgs, cut, into=None):
    args = (measured, mask, *msgs) + (() if into is None else (into,))
    (out,) = call(
        functools.partial(unpack_kernel, cut, d),
        "unpack",
        args,
        [jax.ShapeDtypeStruct(measured.shape, F32)],
        [pltpu.VMEM((cut.ch, cut.G, cut.D, cut.W), F32), pltpu.SemaphoreType.DMA((cut.G // 2,))],
        far=() if into is None else (len(args) - 1,),
        out=ANY,
        input_output_aliases={} if into is None else {len(args) - 1: 0},
    )
    return out


def on_device(measured, mask, kernel):
    Z, C, X = (lax.axis_size(axis) for axis in AXES)
    every = [(z, c, x) for z in range(Z) for c in range(C) for x in range(X)]

    def index(z, c, x):
        return (z * C + c) * X + x

    def send(array, target):
        return lax.ppermute(array, AXES, [(index(*p), index(*target(*p))) for p in every])

    def exchange(msgs):
        got = list(msgs)
        for d in range(C):
            got[2 * d + 1] = send(msgs[2 * d + 1], lambda z, c, x: (Z - 1 - z, c ^ d, X - 1 - x))
        for d in range(1, C):
            got[2 * d] = send(msgs[2 * d], lambda z, c, x: (z, c ^ d, x))
        return got

    def plane_a(z, c, x):
        return (z ^ 1, c, x)

    def plane_b(z, c, x):
        other = z + 1 if z % 2 else z - 1
        return (other, c, x) if 0 <= other < Z else (z, c, X - 1 - x)

    def core(z, c, x):
        return (z, c, X - 1 - x)

    parts, coils, rows, D, W = measured.shape
    cut = Cut(rows, D, W, C, 2 * parts * coils * C)
    flat = measured.reshape(parts * coils, rows, D, W)
    kernel = kernel.reshape(-1, *kernel.shape[2:])
    msgs = []
    for d in reversed(range(C)):
        msgs = [*pack(d, flat, mask, cut), *msgs]
        kernel, mask, *msgs = lax.optimization_barrier((kernel, mask, *msgs)) if d else (kernel, mask, *msgs)
    msgs = exchange(msgs)
    folded = []
    for d in range(1, C):
        half = send(fold(kernel), lambda z, c, x: (z, c ^ d, x))
        folded += [half, send(half, core)]
    weights = build_weights(kernel, folded, cut)
    state, marks, edge, near, added = points(cut, weights, msgs, lambda row: send(row, core))
    near = send(near, core)
    got = [send(face, to) for face, to in zip(faces(state, near, cut), (plane_a, plane_b))]
    main = inside_half(1, state, weights, cut, near, added)
    face = jax.ShapeDtypeStruct(((cut.G + 2) * cut.V, cut.channels), F32)
    state, *sides = call(
        functools.partial(middle_kernel, cut),
        "middle",
        (state, marks, edge, near, main, *got, *weights),
        [jax.ShapeDtypeStruct(main.shape, F32), face, face],
        [planes_scratch(cut, cut.G + 2)],
    )
    got = [send(face, to) for face, to in zip(sides[::-1], (plane_b, plane_a))]
    main = inside(state, weights, cut)
    message = jax.ShapeDtypeStruct((cut.ch * D, cut.G * cut.H), F32)
    msgs = call(
        functools.partial(last_kernel, cut),
        "last",
        (main, *got, *weights),
        [message] * (2 * C),
        [pltpu.VMEM(main.shape, F32), pltpu.VMEM((cut.channels * D, cut.G * cut.H), F32), planes_scratch(cut, cut.G)],
    )
    msgs = exchange(msgs)
    out = None
    for d in reversed(range(C)):
        out = unpack(d, flat, mask, (msgs[2 * d + 1], msgs[2 * d]), cut, out)
    return out.reshape(measured.shape)


def solution(mesh):
    placed = (
        P(None, ("grp", "coil"), "kx", "kz", None),
        P(("grp", "kx"), "kz", None),
        P(None, None, "coil", None),
    )
    return jax.shard_map(
        on_device,
        mesh=mesh,
        in_specs=placed,
        out_specs=P(None, ("grp", "coil"), "kx", "kz", None),
        check_vma=False,
    )
```
